256 devices in a mesh: group: 16 (over x_hi, z), fsdp: 16 (over y, x_lo, core).
Axes of the slice: x: 4 (x_hi: 2, x_lo: 2; x = x_hi * 2 + x_lo), y: 4, z: 8, core: 2. Of those that a mesh axis runs over, the one named last changes fastest.
Arguments:
- activations: bfloat16 [16, 4096, 8192], P('group', 'fsdp'), may hold values from -6 to 6
- targets: bfloat16 [16, 4096, 512], P('group', 'fsdp'), may hold values from -6 to 6
- token_ids: int32 [16, 4096], P('group', 'fsdp'), may hold values from 0 to 128255, as said below
- sync_fragment: int32 [4], replicated, may hold values from 0 to 3, each once
- params: float32 [16, 8192, 512], P('group', 'fsdp'), may hold values from -6 to 6
- adam_m: float32 [16, 8192, 512], P('group', 'fsdp'), may hold values from -0.0007324219 to 0.0007324219
- adam_v: float32 [16, 8192, 512], P('group', 'fsdp'), may hold values from 7.450581e-09 to 1.1920929e-07
- anchor: float32 [8192, 512], P('fsdp'), may hold values from -6 to 6
- momentum: float32 [8192, 512], P('fsdp'), may hold values from -4 to 4
Outputs:
- new_params: float32 [16, 8192, 512], P('group', 'fsdp')
- new_adam_m: float32 [16, 8192, 512], P('group', 'fsdp')
- new_adam_v: float32 [16, 8192, 512], P('group', 'fsdp')
- new_anchor: float32 [8192, 512], P('fsdp')
- new_momentum: float32 [8192, 512], P('fsdp')
The draws below stay inside these ranges and needn't reach their ends.
Inputs may be any that keep to these rules, and one draw needn't show every extreme that they name: `token_ids`: 0 marks padding, other values are vocabulary ids; in each aligned block of 256 tokens the padding stands at the end and covers at most three quarters of the block. `sync_fragment`: each fragment appears once.
All inputs are finite; a program needn't handle non-finite values.
Results may differ from the reference program's by a relative error of at most 0.0028.
Values may be sent and summed in bfloat16 or wider, within the bound.
A program may use at most 128 MiB of HBM per device.

```python
import math
import jax
import jax.numpy as jnp
from jax import lax

D = 8192
KV = 512
HEAD = 128
TOK_DEV = 256
FRAGS = 4
TOKENS = 4096
GROUPS = 16
N_GROUP = 16


def draw_token_ids(key, part):
    key = jax.random.fold_in(key, 11)
    length_key, id_key = jax.random.split(key)
    blocks = TOKENS // TOK_DEV
    lengths = jax.random.randint(length_key, (GROUPS, blocks), TOK_DEV // 4, TOK_DEV + 1)
    lengths = lengths.at[0, 0].set(TOK_DEV // 4)
    ids = jax.random.randint(id_key, (GROUPS, TOKENS), 1, 128256)
    ids = ids.at[0, 0].set(128255)
    position = jnp.arange(TOKENS) % TOK_DEV
    block_of = jnp.arange(TOKENS) // TOK_DEV
    keep = position[None, :] < lengths[:, block_of]
    return jnp.where(keep, ids, 0).astype(jnp.int32)


def steps_of(stream_key, extent, cuts, least, largest):
    gain, own = 1.0, jax.random.fold_in(stream_key, 6)
    for dim, blocks in cuts:
        draws = jnp.exp(jax.random.uniform(jax.random.fold_in(own, dim), (blocks,), jnp.float32, least / len(cuts), largest / len(cuts)))
        gain = gain * jnp.repeat(draws, extent[dim] // blocks).reshape([-1 if axis == dim else 1 for axis in range(len(extent))])
    return gain


def noise(stream_key, dims, scale, bound, shards=(), held_as=jnp.bfloat16):
    drawn = jax.random.normal(stream_key, dims, jnp.float32) * scale
    if len(shards) > 0:
        drawn = steps_of(stream_key, dims, shards, -0.22, 0.18) * drawn
    return jnp.clip(drawn, min=-bound, max=bound).astype(held_as)


def setup_inputs(seed: int = 0) -> dict:
    key_list = jax.random.split(jax.random.key(seed), 10)
    activations = noise(key_list[0], (GROUPS, TOKENS, D), 1.0, 6.0, ((0, 16), (1, 16)))
    targets = noise(key_list[1], (GROUPS, TOKENS, KV), 1.0, 6.0, ((0, 16), (1, 16)))
    token_ids = draw_token_ids(jax.random.fold_in(key_list[9], 71), 0)
    sync_fragment = jax.random.permutation(key_list[3], FRAGS).astype(jnp.int32)
    params = noise(key_list[4], (GROUPS, D, KV), 1.0, 6.0, ((0, 16), (1, 16)), jnp.float32)
    adam_m = noise(key_list[5], (GROUPS, D, KV), (0.3 * (TOKENS * D) ** -0.5), 0.0007324219, ((0, 16), (1, 16)), jnp.float32)
    adam_v = jnp.clip(jnp.exp(math.log(1.1920928955078125e-07) - 2.7725887 * jax.random.uniform(key_list[6], (GROUPS, D, KV), jnp.float32) ** steps_of(key_list[6], (GROUPS, D, KV), ((0, 16), (1, 16)), -0.2, 0.2)), 7.450580596923828e-09, 1.1920928955078125e-07)
    anchor = noise(key_list[7], (D, KV), 1.0, 6.0, ((0, 16),), jnp.float32)
    momentum = noise(key_list[8], (D, KV), 0.3, 4.0, ((0, 16),), jnp.float32)
    return dict(activations=activations, targets=targets, token_ids=token_ids, sync_fragment=sync_fragment, params=params, adam_m=adam_m, adam_v=adam_v, anchor=anchor, momentum=momentum)


beta_one = 0.9
beta_two = 0.999
learn_rate = 0.05
decay_rate = 0.1
adam_epsilon = 1e-08
outer_rate = 0.7
outer_beta = 0.9
merge_weight = 0.5

def reference(activations, targets, token_ids, sync_fragment, params, adam_m, adam_v, anchor, momentum):
    scale = float(D) ** (-0.5)
    start = (sync_fragment[0] * HEAD).astype(jnp.int32)
    arrived = (sync_fragment[1] * HEAD).astype(jnp.int32)
    anchor_cols = lax.dynamic_slice_in_dim(anchor, start, HEAD, 1)
    worker_cols = lax.dynamic_slice_in_dim(params, start, HEAD, 2)
    delta = lax.optimization_barrier(jnp.sum(anchor_cols[None] - worker_cols, axis=0)) / N_GROUP
    moment_frag = outer_beta * lax.dynamic_slice_in_dim(momentum, start, HEAD, 1) + delta
    anchor_frag = anchor_cols - outer_rate * (delta + outer_beta * moment_frag)
    new_momentum = lax.dynamic_update_slice_in_dim(momentum, moment_frag, start, 1)
    new_anchor = lax.dynamic_update_slice_in_dim(anchor, anchor_frag, start, 1)
    arrived_cols = lax.dynamic_slice_in_dim(anchor, arrived, HEAD, 1)

    def worker(items):
        inputs, target, ids, weight, first, second = items
        weights = weight.astype(jnp.bfloat16)
        keys = jnp.dot(inputs, weights, preferred_element_type=jnp.float32) * scale
        live = (ids != 0).astype(jnp.float32)
        count = jnp.sum(live)
        resid = (live[:, None] * (keys - target.astype(jnp.float32)) / count).astype(jnp.bfloat16)
        grad = jnp.einsum('tk,tc->kc', inputs, resid, preferred_element_type=jnp.float32) * scale
        first = beta_one * first + (1.0 - beta_one) * grad
        second = beta_two * second + (1.0 - beta_two) * grad * grad
        stepped = weight - learn_rate * (first / (jnp.sqrt(second) + adam_epsilon) + decay_rate * weight)
        merged = merge_weight * lax.dynamic_slice_in_dim(stepped, arrived, HEAD, 1) + (1.0 - merge_weight) * arrived_cols
        return (lax.dynamic_update_slice_in_dim(stepped, merged, arrived, 1), first, second)
    new_params, new_adam_m, new_adam_v = lax.map(worker, (activations, targets, token_ids, params, adam_m, adam_v))
    return (new_params, new_adam_m, new_adam_v, new_anchor, new_momentum)
```

```python
import functools

import jax
import jax.numpy as jnp
from jax import lax
from jax.experimental import pallas as pl
from jax.experimental.pallas import tpu as pltpu
from jax.sharding import PartitionSpec as P

HEAD = 128
MESH = pl.DeviceIdType.MESH
F32 = jnp.float32
BF16 = jnp.bfloat16

beta_one = 0.9
beta_two = 0.999
learn_rate = 0.05
decay_rate = 0.1
adam_epsilon = 1e-08
outer_rate = 0.7
outer_beta = 0.9
merge_weight = 0.5

NF = 16
NZ = 8

(S_OWN, YP_OWN, YM_OWN, X_OWN, YP_F, YM_F, YP_X, YM_X, X_FA, X_FB,
 S_YP, S_YM, S_X, S_YA, S_YB, S_YPX, S_YMX, S_XA, S_XB) = range(19)
GS = 19
X1, Y1P, Y1M, Y2P, Y2M, Y3PB, Y3PA, Y3MA, Y3MB, X2 = range(27, 37)
KINDS = 37


def sync_kernel(scale, act, tgt, ids, frag, params, anchor, grad_out, delta_out,
                xv, xt, tv, pv, av, live, total, wg, gown, gsend, gsib,
                rx1, ry1p, ry1m, ry2p, ry2m, ry3p, ry3m, rx2,
                tx1, ty1p, ty1m, ty2p, ty2m, ty3p, ty3m, tx2,
                gout, dd, zrecv, zs, xrecv, dall, cs, cr,
                ssem, rsem, zsem, zrsem, csem, crsem, lsem):
    nq, _, rows, cw = wg.shape
    tokens = xv.shape[0]
    half = rows // 2
    g, me = lax.axis_index("group"), lax.axis_index("fsdp")
    y, x, c = me // 4, lax.rem(me // 2, 2), lax.rem(me, 2)
    z, far = lax.rem(g, NZ), g // NZ
    yp, ym, y2, xo, co = lax.rem(y + 1, 4), lax.rem(y + 3, 4), lax.rem(y + 2, 4), 1 - x, 1 - c
    groups = lax.axis_size("group")

    def at(yy, xx, cc):
        return yy * 4 + xx * 2 + cc

    def zdev(k):
        return (far * NZ + lax.rem(z + k, NZ), me)

    sib, up, down, side = ((g, at(y, x, co)), (g, at(yp, x, c)), (g, at(ym, x, c)), (g, at(y, xo, c)))
    across = ((1 - far) * NZ + z, me)

    def load(src, dst, k):
        return pltpu.make_async_copy(src, dst, lsem.at[k])

    l_params = load(params.at[0], pv, 0)
    l_params.start()
    l_anchor = load(anchor, av, 1)
    l_anchor.start()
    l_act = load(act.at[0], xv, 2)
    l_act.start()
    l_tgt = load(tgt.at[0], tv, 3)
    l_tgt.start()

    row = jnp.where(ids[...] != 0, 1.0, 0.0).astype(F32)
    live[...] = jnp.transpose(jnp.broadcast_to(row, (HEAD, tokens)))
    cs[0] = jnp.broadcast_to(jnp.sum(row), cs.shape[1:])

    peers = [sib, up, down, side]
    if groups > 1:
        peers += [zdev(k) for k in range(1, NZ)] + [across]
    barrier = pltpu.get_barrier_semaphore()
    for peer in peers:
        pl.semaphore_signal(barrier, inc=1, device_id=peer, device_id_type=MESH)
    l_params.wait()
    for q in range(nq):
        wg[q, me] = pv[:, q * cw:(q + 1) * cw].astype(BF16)
    pl.semaphore_wait(barrier, len(peers))

    sends = []

    def remote(src, dst, q, kind, peer):
        return pltpu.make_async_remote_copy(
            src_ref=src, dst_ref=dst, send_sem=ssem.at[q, kind], recv_sem=rsem.at[q, kind],
            device_id=peer, device_id_type=MESH)

    def send(src, dst, q, kind, peer):
        copy = remote(src, dst, q, kind, peer)
        copy.start()
        sends.append(copy)

    def arrived(dst, q, kind):
        remote(dst, dst, q, kind, sib).wait_recv()

    def part(name):
        return {"a": pl.ds(0, half), "b": pl.ds(half, half), None: pl.ds(0, rows)}[name]

    def gsend_w(q, kind, peer, shard, rng=None):
        ref = wg.at[q, shard, part(rng)]
        send(ref, ref, q, kind, peer)

    def got_w(q, kind, shard, rng=None):
        arrived(wg.at[q, shard, part(rng)], q, kind)

    y1, y3 = y + 1 - 2 * lax.rem(y, 2), 3 - y
    count_peers = [sib, side, (g, at(y1, x, c)), (g, at(y3, x, c))]

    def count_send(k):
        copy = pltpu.make_async_remote_copy(
            src_ref=cs.at[k], dst_ref=cr.at[k], send_sem=csem.at[k], recv_sem=crsem.at[k],
            device_id=count_peers[k], device_id_type=MESH)
        copy.start()
        sends.append(copy)

    def count_step(k):
        pltpu.make_async_remote_copy(
            src_ref=cs.at[k], dst_ref=cr.at[k], send_sem=csem.at[k], recv_sem=crsem.at[k],
            device_id=count_peers[k], device_id_type=MESH).wait_recv()
        s = cs[k] + cr[k]
        if k < 3:
            cs[k + 1] = s
            count_send(k + 1)
        else:
            total[...] = s

    def zcopy(src, dst, k, peer):
        return pltpu.make_async_remote_copy(
            src_ref=src, dst_ref=dst, send_sem=zsem.at[k], recv_sem=zrsem.at[k],
            device_id=peer, device_id_type=MESH)

    def delta_start():
        l_anchor.wait()
        diff = av[:, :cw] - pv[:, :cw]
        for f in range(1, nq):
            cols = slice(f * cw, (f + 1) * cw)
            diff = jnp.where(jnp.full(diff.shape, frag[0]) == f, av[:, cols] - pv[:, cols], diff)
        dd[...] = diff.reshape(dd.shape)
        if groups > 1:
            for k in range(1, NZ):
                copy = zcopy(dd.at[lax.rem(z + k, NZ)], zrecv.at[k - 1], k - 1, zdev(k))
                copy.start()
                sends.append(copy)

    def delta_sum():
        if groups > 1:
            s = dd[z]
            for k in range(1, NZ):
                zcopy(zrecv.at[k - 1], zrecv.at[k - 1], k - 1, zdev(k)).wait_recv()
            for k in range(1, NZ):
                s = s + zrecv[k - 1]
            zs[...] = s
            copy = zcopy(zs, xrecv, NZ - 1, across)
            copy.start()
            sends.append(copy)

    def delta_share():
        if groups > 1:
            zcopy(zs, xrecv, NZ - 1, across).wait_recv()
            dall[z] = (zs[...] + xrecv[...]) / groups
            for k in range(1, NZ):
                copy = zcopy(dall.at[z], dall.at[z], NZ + k - 1, zdev(k))
                copy.start()
                sends.append(copy)
        else:
            dall[...] = dd[...]

    def delta_end():
        if groups > 1:
            for k in range(1, NZ):
                slot = dall.at[lax.rem(z + NZ - k, NZ)]
                zcopy(slot, slot, NZ + k - 1, zdev(k)).wait_recv()
        load(dall, delta_out, 4).start()

    def gather_own(q):
        own = at(y, x, c)
        gsend_w(q, YP_OWN, up, own)
        gsend_w(q, YM_OWN, down, own)
        gsend_w(q, X_OWN, side, own)
        gsend_w(q, S_OWN, sib, own)

    def gather_one(q):
        got_w(q, X_OWN, at(y, xo, c))
        gsend_w(q, YP_X, up, at(y, xo, c))
        gsend_w(q, YM_X, down, at(y, xo, c))
        gsend_w(q, S_X, sib, at(y, xo, c))
        got_w(q, YP_OWN, at(ym, x, c))
        gsend_w(q, YP_F, up, at(ym, x, c), "a")
        gsend_w(q, S_YP, sib, at(ym, x, c))
        got_w(q, YM_OWN, at(yp, x, c))
        gsend_w(q, YM_F, down, at(yp, x, c), "b")
        gsend_w(q, S_YM, sib, at(yp, x, c))

    def gather_two(q):
        got_w(q, YP_F, at(y2, x, c), "a")
        gsend_w(q, X_FA, side, at(y2, x, c), "a")
        gsend_w(q, S_YA, sib, at(y2, x, c), "a")
        got_w(q, YM_F, at(y2, x, c), "b")
        gsend_w(q, X_FB, side, at(y2, x, c), "b")
        gsend_w(q, S_YB, sib, at(y2, x, c), "b")

    def gather_three(q):
        got_w(q, YP_X, at(ym, xo, c))
        gsend_w(q, S_YPX, sib, at(ym, xo, c))
        got_w(q, YM_X, at(yp, xo, c))
        gsend_w(q, S_YMX, sib, at(yp, xo, c))
        got_w(q, X_FA, at(y2, xo, c), "a")
        gsend_w(q, S_XA, sib, at(y2, xo, c), "a")
        got_w(q, X_FB, at(y2, xo, c), "b")
        gsend_w(q, S_XB, sib, at(y2, xo, c), "b")

    def gather_end(q):
        got_w(q, S_OWN, at(y, x, co))
        got_w(q, S_X, at(y, xo, co))
        got_w(q, S_YP, at(ym, x, co))
        got_w(q, S_YM, at(yp, x, co))
        got_w(q, S_YA, at(y2, x, co), "a")
        got_w(q, S_YB, at(y2, x, co), "b")
        got_w(q, S_YPX, at(ym, xo, co))
        got_w(q, S_YMX, at(yp, xo, co))
        got_w(q, S_XA, at(y2, xo, co), "a")
        got_w(q, S_XB, at(y2, xo, co), "b")

    order = [(y2, xo), (yp, xo), (ym, xo), (y2, x), (yp, x), (ym, x), (y, xo), (y, x)]

    def compute(q):
        def body(i, acc):
            cols = pl.ds(pl.multiple_of(i * rows, rows), rows)
            return acc + jnp.dot(xv[:, cols], wg[q, i], preferred_element_type=F32)

        keys = lax.fori_loop(0, NF, body, jnp.zeros((tokens, cw), F32)) * scale
        target = tv[:, q * cw:(q + 1) * cw].astype(F32)
        resid = (live[...] * (keys - target) / total[0:1, 0:1]).astype(BF16)
        for j, (yy, xx) in enumerate(order):
            gsend[q, j] = jnp.dot(xt[at(yy, xx, co)], resid, preferred_element_type=F32).astype(BF16)
            send(gsend.at[q, j], gsib.at[q, j], q, GS + j, sib)
        for j, (yy, xx) in enumerate(order):
            gown[q, j] = jnp.dot(xt[at(yy, xx, c)], resid, preferred_element_type=F32)

    lo, hi = slice(0, half), slice(half, rows)

    def got_s(q, j):
        arrived(gsib.at[q, j], q, GS + j)

    def pair(q, j, rng=slice(None)):
        return gown[q, j, rng] + gsib[q, j, rng].astype(F32)

    def scatter_one(q):
        for j, buf, dst, kind, peer in ((0, tx1, rx1, X1, side), (1, ty1p, ry1p, Y1P, up), (2, ty1m, ry1m, Y1M, down)):
            got_s(q, j)
            buf[q] = pair(q, j).astype(BF16)
            send(buf.at[q], dst.at[q], q, kind, peer)
        got_s(q, 3)
        got_s(q, 4)
        ty3p[q, hi] = pair(q, 4, hi).astype(BF16)
        send(ty3p.at[q, part("b")], ry3p.at[q, part("b")], q, Y3PB, up)
        got_s(q, 5)
        ty3m[q, lo] = pair(q, 5, lo).astype(BF16)
        send(ty3m.at[q, part("a")], ry3m.at[q, part("a")], q, Y3MA, down)
        got_s(q, 6)
        got_s(q, 7)

    def scatter_two(q):
        arrived(rx1.at[q], q, X1)
        ty2p[q] = (pair(q, 3, lo) + rx1[q, lo].astype(F32)).astype(BF16)
        send(ty2p.at[q], ry2p.at[q], q, Y2P, up)
        ty2m[q] = (pair(q, 3, hi) + rx1[q, hi].astype(F32)).astype(BF16)
        send(ty2m.at[q], ry2m.at[q], q, Y2M, down)
        arrived(ry1p.at[q], q, Y1P)
        arrived(ry1m.at[q], q, Y1M)
        tx2[q] = (pair(q, 6) + ry1p[q].astype(F32) + ry1m[q].astype(F32)).astype(BF16)
        send(tx2.at[q], rx2.at[q], q, X2, side)

    def scatter_three(q):
        arrived(ry2p.at[q], q, Y2P)
        ty3p[q, lo] = (pair(q, 4, lo) + ry2p[q].astype(F32)).astype(BF16)
        send(ty3p.at[q, part("a")], ry3p.at[q, part("a")], q, Y3PA, up)
        arrived(ry2m.at[q], q, Y2M)
        ty3m[q, hi] = (pair(q, 5, hi) + ry2m[q].astype(F32)).astype(BF16)
        send(ty3m.at[q, part("b")], ry3m.at[q, part("b")], q, Y3MB, down)

    def out_copy(q):
        cols = pl.ds(q * cw, cw)
        return pltpu.make_async_copy(gout.at[:, cols], grad_out.at[:, cols], lsem.at[5 + q])

    def scatter_end(q):
        arrived(rx2.at[q], q, X2)
        arrived(ry3p.at[q, part("b")], q, Y3PB)
        arrived(ry3m.at[q, part("a")], q, Y3MA)
        arrived(ry3p.at[q, part("a")], q, Y3PA)
        arrived(ry3m.at[q, part("b")], q, Y3MB)
        s = pair(q, 7) + rx2[q].astype(F32) + ry3p[q].astype(F32) + ry3m[q].astype(F32)
        gout[:, q * cw:(q + 1) * cw] = s * scale
        out_copy(q).start()

    count_send(0)
    gather_own(0)
    gather_own(1)
    count_step(0)
    delta_start()
    l_act.wait()

    def turn(i):
        cols = pl.ds(pl.multiple_of(i * rows, rows), rows)
        xt[i] = jnp.transpose(xv[:, cols])

    def turn_some(first, last):
        def body(i, carry):
            turn(i)
            return carry
        lax.fori_loop(first, last, body, 0)

    turn_some(0, 4)
    count_step(1)
    gather_one(0)
    gather_own(2)
    turn_some(4, 8)
    count_step(2)
    gather_one(1)
    gather_own(3)
    turn_some(8, 12)
    gather_two(0)
    gather_one(2)
    turn_some(12, 16)
    gather_three(0)
    gather_two(1)
    gather_one(3)
    count_step(3)
    delta_sum()
    l_tgt.wait()
    gather_end(0)
    compute(0)
    gather_three(1)
    gather_two(2)
    scatter_one(0)
    gather_end(1)
    compute(1)
    gather_three(2)
    gather_two(3)
    scatter_two(0)
    scatter_one(1)
    delta_share()
    gather_end(2)
    compute(2)
    gather_three(3)
    scatter_three(0)
    scatter_two(1)
    scatter_one(2)
    gather_end(3)
    compute(3)
    scatter_three(1)
    scatter_two(2)
    scatter_one(3)
    scatter_end(0)
    scatter_three(2)
    scatter_two(3)
    scatter_end(1)
    delta_end()
    scatter_three(3)
    scatter_end(2)
    scatter_end(3)
    for copy in sends:
        copy.wait_send()
    load(dall, delta_out, 4).wait()
    for q in range(nq):
        out_copy(q).wait()


def sync(activations, targets, token_ids, sync_fragment, params, anchor):
    tokens, width = activations.shape[1:]
    rows, kv = params.shape[1:]
    nq = kv // HEAD
    piece = (nq, rows, HEAD)
    part = (nq, rows // 2, HEAD)
    anywhere = pl.BlockSpec(memory_space=pl.ANY)
    return pl.pallas_call(
        functools.partial(sync_kernel, float(width) ** (-0.5)),
        out_shape=(jax.ShapeDtypeStruct((rows, kv), F32), jax.ShapeDtypeStruct((NZ, rows // NZ, HEAD), F32)),
        in_specs=[anywhere, anywhere, pl.BlockSpec(memory_space=pltpu.VMEM), pl.BlockSpec(memory_space=pltpu.SMEM), anywhere, anywhere],
        out_specs=(anywhere, anywhere),
        scratch_shapes=[
            pltpu.VMEM((tokens, width), BF16),
            pltpu.VMEM((NF, rows, tokens), BF16),
            pltpu.VMEM((tokens, kv), BF16),
            pltpu.VMEM((rows, kv), F32),
            pltpu.VMEM((rows, kv), F32),
            pltpu.VMEM((tokens, HEAD), F32),
            pltpu.VMEM((8, HEAD), F32),
            pltpu.VMEM((nq, NF, rows, HEAD), BF16),
            pltpu.VMEM((nq, 8, rows, HEAD), F32),
            pltpu.VMEM((nq, 8, rows, HEAD), BF16),
            pltpu.VMEM((nq, 8, rows, HEAD), BF16),
            pltpu.VMEM(piece, BF16), pltpu.VMEM(piece, BF16), pltpu.VMEM(piece, BF16),
            pltpu.VMEM(part, BF16), pltpu.VMEM(part, BF16),
            pltpu.VMEM(piece, BF16), pltpu.VMEM(piece, BF16), pltpu.VMEM(piece, BF16),
            pltpu.VMEM(piece, BF16), pltpu.VMEM(piece, BF16), pltpu.VMEM(piece, BF16),
            pltpu.VMEM(part, BF16), pltpu.VMEM(part, BF16),
            pltpu.VMEM(piece, BF16), pltpu.VMEM(piece, BF16), pltpu.VMEM(piece, BF16),
            pltpu.VMEM((rows, kv), F32),
            pltpu.VMEM((NZ, rows // NZ, HEAD), F32),
            pltpu.VMEM((NZ - 1, rows // NZ, HEAD), F32),
            pltpu.VMEM((rows // NZ, HEAD), F32),
            pltpu.VMEM((rows // NZ, HEAD), F32),
            pltpu.VMEM((NZ, rows // NZ, HEAD), F32),
            pltpu.VMEM((4, 8, HEAD), F32),
            pltpu.VMEM((4, 8, HEAD), F32),
            pltpu.SemaphoreType.DMA((nq, KINDS)),
            pltpu.SemaphoreType.DMA((nq, KINDS)),
            pltpu.SemaphoreType.DMA((2 * NZ,)),
            pltpu.SemaphoreType.DMA((2 * NZ,)),
            pltpu.SemaphoreType.DMA((4,)),
            pltpu.SemaphoreType.DMA((4,)),
            pltpu.SemaphoreType.DMA((5 + nq,)),
        ],
        compiler_params=pltpu.CompilerParams(
            collective_id=0, has_side_effects=True, vmem_limit_bytes=54 * 2**20
        ),
        cost_estimate=pl.CostEstimate(
            flops=4 * tokens * width * kv, bytes_accessed=2 * tokens * width + 12 * rows * kv, transcendentals=0
        ),
        name="sync",
    )(activations, targets, token_ids, sync_fragment, params, anchor)


def update_kernel(frag, grad, delta, params, adam_m, adam_v, anchor, momentum,
                  new_params, new_m, new_v, new_anchor, new_momentum):
    fragment = pl.ds(pl.multiple_of(frag[0] * HEAD, HEAD), HEAD)
    arriving = pl.ds(pl.multiple_of(frag[1] * HEAD, HEAD), HEAD)
    slope = grad[...]
    weight = params[...]
    first = beta_one * adam_m[...] + (1.0 - beta_one) * slope
    second = beta_two * adam_v[...] + (1.0 - beta_two) * slope * slope
    new_m[...] = first
    new_v[...] = second
    new_params[...] = weight - learn_rate * (first / (jnp.sqrt(second) + adam_epsilon) + decay_rate * weight)
    new_params[:, arriving] = merge_weight * new_params[:, arriving] + (1.0 - merge_weight) * anchor[:, arriving]
    new_anchor[...] = anchor[...]
    new_momentum[...] = momentum[...]
    change = delta[...]
    moment = outer_beta * momentum[:, fragment] + change
    new_momentum[:, fragment] = moment
    new_anchor[:, fragment] = anchor[:, fragment] - outer_rate * (change + outer_beta * moment)


def update(frag, grad, delta, params, adam_m, adam_v, anchor, momentum, steps=4):
    rows, kv = grad.shape
    size = rows // steps
    worker = pl.BlockSpec((None, size, kv), lambda i: (0, i, 0))
    shared = pl.BlockSpec((size, kv), lambda i: (i, 0))
    strip = pl.BlockSpec((size, HEAD), lambda i: (i, 0))
    return pl.pallas_call(
        update_kernel,
        grid=(steps,),
        out_shape=[jax.ShapeDtypeStruct((1, rows, kv), F32)] * 3 + [jax.ShapeDtypeStruct((rows, kv), F32)] * 2,
        in_specs=[pl.BlockSpec(memory_space=pltpu.SMEM), shared, strip, worker, worker, worker, shared, shared],
        out_specs=[worker, worker, worker, shared, shared],
        name="update",
    )(frag, grad, delta, params, adam_m, adam_v, anchor, momentum)


def on_device(activations, targets, token_ids, sync_fragment, params, adam_m, adam_v, anchor, momentum):
    grad, delta = sync(activations, targets, token_ids, sync_fragment, params, anchor)
    delta = delta.reshape(delta.shape[0] * delta.shape[1], delta.shape[2])
    return tuple(update(sync_fragment, grad, delta, params, adam_m, adam_v, anchor, momentum))


def solution(mesh):
    worker = P("group", "fsdp", None)
    shared = P("fsdp", None)
    return jax.shard_map(
        on_device,
        mesh=mesh,
        in_specs=(worker, worker, P("group", "fsdp"), P(), worker, worker, worker, shared, shared),
        out_specs=(worker, worker, worker, shared, shared),
        check_vma=False,
    )
```

```python
import functools

import jax
import jax.numpy as jnp
from jax import lax
from jax.experimental import pallas as pl
from jax.experimental.pallas import tpu as pltpu
from jax.sharding import PartitionSpec as P

HEAD = 128
MESH = pl.DeviceIdType.MESH
F32 = jnp.float32
BF16 = jnp.bfloat16

beta_one = 0.9
beta_two = 0.999
learn_rate = 0.05
decay_rate = 0.1
adam_epsilon = 1e-08
outer_rate = 0.7
outer_beta = 0.9
merge_weight = 0.5

NF = 16
NZ = 8

EDGE = 80

(S_OWN, YP_OWN, YM_OWN, X_OWN, YP_F, YM_F, YP_X, YM_X, X_FA, X_FB, X_P, X_M,
 S_YP, S_YM, S_X, S_YA, S_YB, S_YPX, S_YMX, S_XA, S_XB) = range(21)
GS = 21
X1, Y1P, Y1M, XEP, XEM, Y2P, Y2M, Y3PB, Y3PA, Y3MA, Y3MB, X2 = range(29, 41)
KINDS = 41


def sync_kernel(scale, act, tgt, ids, fragments, params, anchor, grad_out, delta_out,
                frag, xv, xt, tv, pv, av, iv, live, total, wg, acc, gown, gsend, gsib,
                rx1, ry1p, ry1m, rxep, rxem, ry2p, ry2m, ry3p, ry3m, rx2,
                tx1, ty1p, ty1m, ty2p, ty2m, ty3p, ty3m, tx2,
                dd, zrecv, zs, xrecv, cs, cr,
                ssem, rsem, zsem, zrsem, csem, crsem, lsem):
    nq, _, rows, cw = wg.shape
    tokens = xv.shape[0]
    half = rows // 2
    edge = rxep.shape[1]
    g, me = lax.axis_index("group"), lax.axis_index("fsdp")
    y, x, c = me // 4, lax.rem(me // 2, 2), lax.rem(me, 2)
    z, far = lax.rem(g, NZ), g // NZ
    yp, ym, y2, xo, co = lax.rem(y + 1, 4), lax.rem(y + 3, 4), lax.rem(y + 2, 4), 1 - x, 1 - c
    groups = lax.axis_size("group")

    def at(yy, xx, cc):
        return yy * 4 + xx * 2 + cc

    def zdev(k):
        return (far * NZ + lax.rem(z + k, NZ), me)

    sib, up, down, side = ((g, at(y, x, co)), (g, at(yp, x, c)), (g, at(ym, x, c)), (g, at(y, xo, c)))
    across = ((1 - far) * NZ + z, me)

    peers = [sib, up, down, side]
    if groups > 1:
        peers += [zdev(k) for k in range(1, NZ)] + [across]
    barrier = pltpu.get_barrier_semaphore()
    for peer in peers:
        pl.semaphore_signal(barrier, inc=1, device_id=peer, device_id_type=MESH)

    def columns(q):
        return slice(q * cw, (q + 1) * cw)

    def load(src, dst, k):
        copy = pltpu.make_async_copy(src, dst, lsem.at[k])
        copy.start()
        return copy

    l_params = [load(params.at[0, :, columns(q)], pv.at[:, columns(q)], q) for q in range(nq)]
    l_ids = load(ids, iv, nq)
    l_act = load(act.at[0], xv, nq + 1)
    l_tgt = load(tgt.at[0], tv, nq + 2)
    l_anchor = load(anchor, av, nq + 3)
    l_frag = load(fragments, frag, nq + 4)

    sends = {}

    def start(copy, tag=None):
        copy.start()
        sends.setdefault(tag, []).append(copy)

    def settle(tag):
        for copy in sends.pop(tag, []):
            copy.wait_send()

    def settle_gather():
        for q in range(nq):
            settle(-1 - q)

    def remote(src, dst, q, kind, peer):
        return pltpu.make_async_remote_copy(
            src_ref=src, dst_ref=dst, send_sem=ssem.at[q, kind], recv_sem=rsem.at[q, kind],
            device_id=peer, device_id_type=MESH)

    def send(src, dst, q, kind, peer):
        start(remote(src, dst, q, kind, peer), q if kind >= GS else -1 - q)

    def arrived(dst, q, kind):
        remote(dst, dst, q, kind, sib).wait_recv()

    y1, y3 = y + 1 - 2 * lax.rem(y, 2), 3 - y
    count_peers = [sib, side, (g, at(y1, x, c)), (g, at(y3, x, c))]

    def count_copy(k):
        return pltpu.make_async_remote_copy(
            src_ref=cs.at[k], dst_ref=cr.at[k], send_sem=csem.at[k], recv_sem=crsem.at[k],
            device_id=count_peers[k], device_id_type=MESH)

    def count(k):
        if k == 0:
            l_ids.wait()
            row = jnp.where(iv[...] != 0, 1.0, 0.0).astype(F32)
            live[...] = jnp.transpose(jnp.broadcast_to(row, (HEAD, tokens)))
            part = jnp.broadcast_to(jnp.sum(row), cs.shape[1:])
        else:
            count_copy(k - 1).wait_recv()
            part = cs[k - 1] + cr[k - 1]
        if k < 4:
            cs[k] = part
            start(count_copy(k))
        else:
            total[...] = part

    def zcopy(src, dst, k, peer):
        return pltpu.make_async_remote_copy(
            src_ref=src, dst_ref=dst, send_sem=zsem.at[k], recv_sem=zrsem.at[k],
            device_id=peer, device_id_type=MESH)

    def mean_start():
        l_anchor.wait()
        l_frag.wait()
        diff = av[:, columns(0)] - pv[:, columns(0)]
        for f in range(1, nq):
            diff = jnp.where(jnp.full(diff.shape, frag[0]) == f, av[:, columns(f)] - pv[:, columns(f)], diff)
        dd[...] = diff.reshape(dd.shape)
        if groups > 1:
            for k in range(1, NZ):
                start(zcopy(dd.at[lax.rem(z + k, NZ)], zrecv.at[k - 1], k - 1, zdev(k)))

    def mean_sum():
        if groups > 1:
            for k in range(1, NZ):
                zcopy(zrecv.at[k - 1], zrecv.at[k - 1], k - 1, zdev(k)).wait_recv()
            s = dd[z]
            for k in range(1, NZ):
                s = s + zrecv[k - 1]
            zs[...] = s
            start(zcopy(zs, xrecv, NZ - 1, across))

    def mean_share():
        if groups > 1:
            zcopy(zs, xrecv, NZ - 1, across).wait_recv()
            delta_out[z] = (zs[...] + xrecv[...]) / groups
            for k in range(1, NZ):
                start(zcopy(delta_out.at[z], delta_out.at[z], NZ + k - 1, zdev(k)))
        else:
            delta_out[...] = dd[...]

    def mean_end():
        if groups > 1:
            for k in range(1, NZ):
                slot = delta_out.at[lax.rem(z + NZ - k, NZ)]
                zcopy(slot, slot, NZ + k - 1, zdev(k)).wait_recv()

    every, lo, hi = pl.ds(0, rows), pl.ds(0, half), pl.ds(half, half)
    first, but_first = pl.ds(0, edge), pl.ds(edge, rows - edge)
    last, but_last = pl.ds(rows - edge, edge), pl.ds(0, rows - edge)

    def give(q, kind, peer, shard, rng=every):
        ref = wg.at[q, shard, rng]
        send(ref, ref, q, kind, peer)

    def got(q, kind, shard, rng=every):
        arrived(wg.at[q, shard, rng], q, kind)

    def own(q):
        l_params[q].wait()
        wg[q, me] = pv[:, columns(q)].astype(BF16)
        give(q, X_OWN, side, me)
        give(q, YP_OWN, up, me)
        give(q, YM_OWN, down, me)
        give(q, S_OWN, sib, me)

    def from_side(q):
        shard = at(y, xo, c)
        got(q, X_OWN, shard)
        give(q, YP_X, up, shard, but_first)
        give(q, YM_X, down, shard, but_last)
        give(q, S_X, sib, shard)

    def from_down(q):
        shard = at(ym, x, c)
        got(q, YP_OWN, shard)
        give(q, YP_F, up, shard, lo)
        give(q, X_P, side, shard, first)
        give(q, S_YP, sib, shard)

    def from_up(q):
        shard = at(yp, x, c)
        got(q, YM_OWN, shard)
        give(q, YM_F, down, shard, hi)
        give(q, X_M, side, shard, last)
        give(q, S_YM, sib, shard)

    def far_lo(q):
        shard = at(y2, x, c)
        got(q, YP_F, shard, lo)
        give(q, X_FA, side, shard, lo)
        give(q, S_YA, sib, shard, lo)

    def far_hi(q):
        shard = at(y2, x, c)
        got(q, YM_F, shard, hi)
        give(q, X_FB, side, shard, hi)
        give(q, S_YB, sib, shard, hi)

    def corner_down(q):
        shard = at(ym, xo, c)
        got(q, YP_X, shard, but_first)
        got(q, X_P, shard, first)
        give(q, S_YPX, sib, shard)

    def corner_up(q):
        shard = at(yp, xo, c)
        got(q, YM_X, shard, but_last)
        got(q, X_M, shard, last)
        give(q, S_YMX, sib, shard)

    def cross_lo(q):
        shard = at(y2, xo, c)
        got(q, X_FA, shard, lo)
        give(q, S_XA, sib, shard, lo)

    def cross_hi(q):
        shard = at(y2, xo, c)
        got(q, X_FB, shard, hi)
        give(q, S_XB, sib, shard, hi)

    near, distant = [(y, x), (ym, x), (yp, x), (y, xo)], [(y2, x), (ym, xo), (yp, xo), (y2, xo)]

    def product(q, chips, core):
        s = None
        for yy, xx in chips:
            i = at(yy, xx, core)
            cols = pl.ds(pl.multiple_of(i * rows, rows), rows)
            d = jnp.dot(xv[:, cols], wg[q, i], preferred_element_type=F32)
            s = d if s is None else s + d
        return s

    def keys_a(q):
        acc[q] = product(q, near, c)

    def keys_b(q):
        got(q, S_OWN, at(y, x, co))
        got(q, S_X, at(y, xo, co))
        got(q, S_YP, at(ym, x, co))
        got(q, S_YM, at(yp, x, co))
        acc[q] += product(q, near, co)

    def keys_c(q):
        acc[q] += product(q, distant, c)

    resid = {}

    def keys_d(q):
        got(q, S_YA, at(y2, x, co), lo)
        got(q, S_YB, at(y2, x, co), hi)
        got(q, S_YPX, at(ym, xo, co))
        got(q, S_YMX, at(yp, xo, co))
        got(q, S_XA, at(y2, xo, co), lo)
        got(q, S_XB, at(y2, xo, co), hi)
        keys = (acc[q] + product(q, distant, co)) * scale
        target = tv[:, columns(q)].astype(F32)
        resid[q] = (live[...] * (keys - target) / total[0:1, 0:1]).astype(BF16)

    def turn(i):
        for k in (2 * i, 2 * i + 1):
            xt[k] = jnp.transpose(xv[:, k * rows:(k + 1) * rows])

    order = [(y2, xo), (yp, xo), (ym, xo), (y2, x), (yp, x), (ym, x), (y, xo), (y, x)]

    def slope(j, core, q):
        yy, xx = order[j]
        return jnp.dot(xt[at(yy, xx, core)], resid[q], preferred_element_type=F32)

    def theirs(j, q):
        gsend[q, j] = slope(j, co, q).astype(BF16)
        send(gsend.at[q, j], gsib.at[q, j], q, GS + j, sib)

    def ours(j, q):
        gown[q, j] = slope(j, c, q)

    def pair(q, j, rng=every):
        return gown[q, j, rng] + gsib[q, j, rng].astype(F32)

    def pass_on(q, buf, dst, rng, value, kind, peer):
        buf[q, rng] = value.astype(BF16)
        send(buf.at[q, rng], dst.at[q, rng], q, kind, peer)

    def sum_cross(q):
        arrived(gsib.at[q, 0], q, GS)
        pass_on(q, tx1, rx1, every, pair(q, 0), X1, side)

    def sum_corner_up(q):
        arrived(gsib.at[q, 1], q, GS + 1)
        ty1p[q] = pair(q, 1).astype(BF16)
        send(ty1p.at[q, but_first], ry1p.at[q, but_first], q, Y1P, up)
        send(ty1p.at[q, first], rxep.at[q], q, XEP, side)

    def sum_corner_down(q):
        arrived(gsib.at[q, 2], q, GS + 2)
        ty1m[q] = pair(q, 2).astype(BF16)
        send(ty1m.at[q, but_last], ry1m.at[q, but_last], q, Y1M, down)
        send(ty1m.at[q, last], rxem.at[q], q, XEM, side)

    def sum_up(q):
        arrived(gsib.at[q, 4], q, GS + 4)
        pass_on(q, ty3p, ry3p, hi, pair(q, 4, hi), Y3PB, up)

    def sum_down(q):
        arrived(gsib.at[q, 5], q, GS + 5)
        pass_on(q, ty3m, ry3m, lo, pair(q, 5, lo), Y3MA, down)

    def sum_far(q):
        arrived(gsib.at[q, 3], q, GS + 3)
        arrived(rx1.at[q], q, X1)
        s = pair(q, 3) + rx1[q].astype(F32)
        pass_on(q, ty2p, ry2p, pl.ds(0, half), s[:half], Y2P, up)
        pass_on(q, ty2m, ry2m, pl.ds(0, half), s[half:], Y2M, down)

    def sum_side(q):
        arrived(gsib.at[q, 6], q, GS + 6)
        arrived(ry1p.at[q, but_first], q, Y1P)
        arrived(ry1m.at[q, but_last], q, Y1M)
        s = pair(q, 6)
        zero = jnp.zeros((edge, cw), F32)
        s = s + jnp.concatenate([zero, ry1p[q, but_first].astype(F32)])
        s = s + jnp.concatenate([ry1m[q, but_last].astype(F32), zero])
        pass_on(q, tx2, rx2, every, s, X2, side)

    def sum_up_far(q):
        arrived(ry2p.at[q], q, Y2P)
        arrived(rxep.at[q], q, XEP)
        s = pair(q, 4, lo) + ry2p[q].astype(F32)
        s = s + jnp.concatenate([rxep[q].astype(F32), jnp.zeros((half - edge, cw), F32)])
        pass_on(q, ty3p, ry3p, lo, s, Y3PA, up)

    def sum_down_far(q):
        arrived(ry2m.at[q], q, Y2M)
        arrived(rxem.at[q], q, XEM)
        s = pair(q, 5, hi) + ry2m[q].astype(F32)
        s = s + jnp.concatenate([jnp.zeros((half - edge, cw), F32), rxem[q].astype(F32)])
        pass_on(q, ty3m, ry3m, hi, s, Y3MB, down)

    def finish(q):
        arrived(gsib.at[q, 7], q, GS + 7)
        arrived(rx2.at[q], q, X2)
        arrived(ry3p.at[q, hi], q, Y3PB)
        arrived(ry3m.at[q, lo], q, Y3MA)
        arrived(ry3p.at[q, lo], q, Y3PA)
        arrived(ry3m.at[q, hi], q, Y3MB)
        s = pair(q, 7) + rx2[q].astype(F32) + ry3p[q].astype(F32) + ry3m[q].astype(F32)
        grad_out[:, columns(q)] = s * scale

    pl.semaphore_wait(barrier, len(peers))
    own(0)
    count(0)
    count(1)
    own(1)
    own(2)
    from_up(0)
    l_act.wait()
    turn(6)
    from_down(0)
    from_up(1)
    count(2)
    turn(5)
    from_side(0)
    keys_a(0)
    from_down(1)
    own(3)
    from_down(2)
    mean_start()
    far_lo(0)
    count(3)
    far_hi(0)
    turn(0)
    from_up(2)
    from_side(1)
    from_side(2)
    turn(7)
    turn(1)
    keys_a(2)
    far_hi(1)
    corner_down(0)
    keys_b(0)
    keys_a(1)
    far_lo(1)
    keys_b(2)
    turn(4)
    cross_lo(0)
    corner_up(0)
    turn(2)
    keys_b(1)
    cross_hi(0)
    from_up(3)
    turn(3)
    from_down(3)
    count(4)
    keys_c(0)
    from_side(3)
    far_lo(2)
    cross_hi(1)
    l_tgt.wait()
    keys_d(0)
    theirs(0, 0)
    theirs(1, 0)
    ours(0, 0)
    far_hi(2)
    keys_a(3)
    theirs(2, 0)
    ours(2, 0)
    sum_cross(0)
    corner_up(1)
    cross_lo(1)
    corner_down(1)
    keys_c(1)
    ours(3, 0)
    ours(4, 0)
    ours(1, 0)
    theirs(3, 0)
    sum_corner_down(0)
    theirs(4, 0)
    sum_corner_up(0)
    corner_down(2)
    corner_up(2)
    keys_d(1)
    theirs(0, 1)
    ours(1, 1)
    theirs(5, 0)
    cross_hi(2)
    cross_lo(2)
    far_hi(3)
    keys_c(2)
    theirs(1, 1)
    ours(5, 1)
    ours(5, 0)
    far_lo(3)
    ours(0, 1)
    theirs(2, 1)
    keys_d(2)
    sum_far(0)
    corner_up(3)
    sum_cross(1)
    theirs(0, 2)
    sum_corner_up(1)
    sum_down(0)
    theirs(1, 2)
    theirs(3, 1)
    ours(2, 2)
    ours(2, 1)
    sum_corner_down(1)
    ours(4, 2)
    ours(4, 1)
    sum_up(0)
    theirs(2, 2)
    corner_down(3)
    theirs(4, 1)
    ours(3, 1)
    keys_b(3)
    cross_hi(3)
    cross_lo(3)
    theirs(5, 1)
    keys_c(3)
    mean_sum()
    sum_corner_down(2)
    ours(0, 2)
    sum_cross(2)
    sum_up(1)
    ours(1, 2)
    keys_d(3)
    sum_up_far(0)
    theirs(0, 3)
    sum_down_far(0)
    ours(5, 3)
    ours(1, 3)
    ours(0, 3)
    sum_far(1)
    theirs(6, 1)
    theirs(3, 2)
    ours(5, 2)
    theirs(4, 2)
    theirs(6, 0)
    sum_cross(3)
    theirs(5, 2)
    ours(7, 3)
    sum_corner_up(2)
    ours(6, 0)
    mean_share()
    sum_down(1)
    theirs(1, 3)
    ours(2, 3)
    ours(6, 2)
    ours(7, 1)
    ours(3, 2)
    sum_far(2)
    theirs(2, 3)
    theirs(6, 2)
    sum_side(0)
    theirs(3, 3)
    sum_corner_up(3)
    theirs(4, 3)
    ours(3, 3)
    ours(6, 1)
    sum_up_far(1)
    theirs(5, 3)
    sum_corner_down(3)
    settle_gather()
    sum_far(3)
    theirs(6, 3)
    sum_down_far(1)
    theirs(7, 1)
    sum_up(2)
    ours(6, 3)
    theirs(7, 3)
    ours(4, 3)
    sum_side(1)
    sum_side(3)
    sum_down(3)
    ours(7, 2)
    sum_down_far(3)
    mean_end()
    sum_up(3)
    sum_up_far(3)
    sum_down(2)
    sum_up_far(2)
    sum_side(2)
    sum_down_far(2)
    ours(7, 0)
    theirs(7, 0)
    finish(1)
    settle(1)
    theirs(7, 2)
    finish(0)
    settle(0)
    finish(3)
    settle(3)
    finish(2)
    for tag in list(sends):
        settle(tag)


def sync(activations, targets, token_ids, sync_fragment, params, anchor):
    tokens, width = activations.shape[1:]
    rows, kv = params.shape[1:]
    nq = kv // HEAD
    edge = EDGE * rows // 512
    piece = pltpu.VMEM((nq, rows, HEAD), BF16)
    part = pltpu.VMEM((nq, rows // 2, HEAD), BF16)
    thin = pltpu.VMEM((nq, edge, HEAD), BF16)
    block = pltpu.VMEM((rows // NZ, HEAD), F32)
    hbm = pl.BlockSpec(memory_space=pltpu.HBM)
    vmem = pl.BlockSpec(memory_space=pltpu.VMEM)
    return pl.pallas_call(
        functools.partial(sync_kernel, float(width) ** (-0.5)),
        out_shape=(jax.ShapeDtypeStruct((rows, kv), F32), jax.ShapeDtypeStruct((NZ, rows // NZ, HEAD), F32)),
        in_specs=[hbm] * 6,
        out_specs=(vmem, vmem),
        scratch_shapes=[
            pltpu.SMEM(sync_fragment.shape, jnp.int32),
            pltpu.VMEM((tokens, width), BF16),
            pltpu.VMEM((NF, rows, tokens), BF16),
            pltpu.VMEM((tokens, kv), BF16),
            pltpu.VMEM((rows, kv), F32),
            pltpu.VMEM((rows, kv), F32),
            pltpu.VMEM((1, tokens), jnp.int32),
            pltpu.VMEM((tokens, HEAD), F32),
            pltpu.VMEM((8, HEAD), F32),
            pltpu.VMEM((nq, NF, rows, HEAD), BF16),
            pltpu.VMEM((nq, tokens, HEAD), F32),
            pltpu.VMEM((nq, 8, rows, HEAD), F32),
            pltpu.VMEM((nq, 8, rows, HEAD), BF16),
            pltpu.VMEM((nq, 8, rows, HEAD), BF16),
            piece, piece, piece, thin, thin, part, part, piece, piece, piece,
            piece, piece, piece, part, part, piece, piece, piece,
            pltpu.VMEM((NZ, rows // NZ, HEAD), F32),
            pltpu.VMEM((NZ - 1, rows // NZ, HEAD), F32),
            block, block,
            pltpu.VMEM((4, 8, HEAD), F32),
            pltpu.VMEM((4, 8, HEAD), F32),
            pltpu.SemaphoreType.DMA((nq, KINDS)),
            pltpu.SemaphoreType.DMA((nq, KINDS)),
            pltpu.SemaphoreType.DMA((2 * NZ,)),
            pltpu.SemaphoreType.DMA((2 * NZ,)),
            pltpu.SemaphoreType.DMA((4,)),
            pltpu.SemaphoreType.DMA((4,)),
            pltpu.SemaphoreType.DMA((nq + 5,)),
        ],
        compiler_params=pltpu.CompilerParams(
            collective_id=0, has_side_effects=True, vmem_limit_bytes=46 * 2**20
        ),
        cost_estimate=pl.CostEstimate(
            flops=4 * tokens * width * kv, bytes_accessed=2 * tokens * width + 12 * rows * kv, transcendentals=0
        ),
        name="sync",
    )(*[
        pltpu.with_memory_space_constraint(a, pltpu.HBM)
        for a in (activations, targets, token_ids, sync_fragment, params, anchor)
    ])


def update_kernel(steps, frag, grad, delta, params, adam_m, adam_v, anchor, momentum,
                  out_params, out_m, out_v, out_anchor, out_momentum,
                  new_params, new_m, new_v, new_anchor, new_momentum, sem):
    rows = grad.shape[0]
    size = rows // steps
    copies = []

    def store(src, dst):
        copy = pltpu.make_async_copy(src, dst, sem.at[len(copies)])
        copy.start()
        copies.append(copy)

    fragment = pl.ds(pl.multiple_of(frag[0] * HEAD, HEAD), HEAD)
    arriving = pl.ds(pl.multiple_of(frag[1] * HEAD, HEAD), HEAD)
    for i in range(steps):
        r = pl.ds(i * size, size)
        slope = grad[r]
        weight = params[0, r]
        first = beta_one * adam_m[0, r] + (1.0 - beta_one) * slope
        second = beta_two * adam_v[0, r] + (1.0 - beta_two) * slope * slope
        new_m[r] = first
        store(new_m.at[r], out_m.at[0, r])
        new_v[r] = second
        store(new_v.at[r], out_v.at[0, r])
        new_params[r] = weight - learn_rate * (first / (jnp.sqrt(second) + adam_epsilon) + decay_rate * weight)
        new_params[r, arriving] = merge_weight * new_params[r, arriving] + (1.0 - merge_weight) * anchor[r, arriving]
        store(new_params.at[r], out_params.at[0, r])
        new_anchor[r] = anchor[r]
        new_momentum[r] = momentum[r]
        change = delta[r]
        moment = outer_beta * momentum[r, fragment] + change
        new_momentum[r, fragment] = moment
        store(new_momentum.at[r], out_momentum.at[r])
        new_anchor[r, fragment] = anchor[r, fragment] - outer_rate * (change + outer_beta * moment)
        store(new_anchor.at[r], out_anchor.at[r])
    for copy in copies:
        copy.wait()


def update(frag, grad, delta, params, adam_m, adam_v, anchor, momentum, steps=4):
    rows, kv = grad.shape
    vmem = pl.BlockSpec(memory_space=pltpu.VMEM)
    hbm = pl.BlockSpec(memory_space=pltpu.HBM)
    return pl.pallas_call(
        functools.partial(update_kernel, steps),
        out_shape=[jax.ShapeDtypeStruct((1, rows, kv), F32)] * 3 + [jax.ShapeDtypeStruct((rows, kv), F32)] * 2,
        in_specs=[pl.BlockSpec(memory_space=pltpu.SMEM)] + [vmem] * 7,
        out_specs=[hbm] * 5,
        scratch_shapes=[pltpu.VMEM((rows, kv), F32)] * 5 + [pltpu.SemaphoreType.DMA((5 * steps,))],
        compiler_params=pltpu.CompilerParams(vmem_limit_bytes=16 * 2**20),
        name="update",
    )(frag, grad, delta, params, adam_m, adam_v, anchor, momentum)


def on_device(activations, targets, token_ids, sync_fragment, params, adam_m, adam_v, anchor, momentum):
    grad, delta = sync(activations, targets, token_ids, sync_fragment, params, anchor)
    delta = delta.reshape(delta.shape[0] * delta.shape[1], delta.shape[2])
    return tuple(update(sync_fragment, grad, delta, params, adam_m, adam_v, anchor, momentum))


def solution(mesh):
    worker = P("group", "fsdp", None)
    shared = P("fsdp", None)
    return jax.shard_map(
        on_device,
        mesh=mesh,
        in_specs=(worker, worker, P("group", "fsdp"), P(), worker, worker, worker, shared, shared),
        out_specs=(worker, worker, worker, shared, shared),
        check_vma=False,
    )
```

```python
import functools

import jax
import jax.numpy as jnp
from jax import lax
from jax.experimental import pallas as pl
from jax.experimental.pallas import tpu as pltpu
from jax.sharding import PartitionSpec as P

HEAD = 128
MESH = pl.DeviceIdType.MESH
F32 = jnp.float32
BF16 = jnp.bfloat16

beta_one = 0.9
beta_two = 0.999
learn_rate = 0.05
decay_rate = 0.1
adam_epsilon = 1e-08
outer_rate = 0.7
outer_beta = 0.9
merge_weight = 0.5

NF = 16
NZ = 8

EDGE = 80

(X_OWN, YP_OWN, YM_OWN, YP_X, YM_X, YP_F, YM_F, X_P, X_M, X_FA, X_FB, KEYS, ROWS,
 X1, Y1P, Y1M, XEP, XEM, Y2P, Y2M, Y3PB, Y3PA, Y3MA, Y3MB, X2) = range(25)
KINDS = 25


def sync_kernel(scale, act, tgt, ids, fragments, params, adam_m, adam_v, anchor, momentum,
                grad_out, delta_out, pv, mv, vv, av, uv,
                frag, xk, xt, tv, iv, live, total, wg, acc, ksend, krecv, rs, gown,
                rx1, ry1p, ry1m, rxep, rxem, ry2p, ry2m, ry3p, ry3m, rx2,
                tx1, ty1p, ty1m, ty2p, ty2m, ty3p, ty3m, tx2,
                dd, sum_b, sum_c, sum_d, from_b, from_c, from_d, from_e, cs, cr,
                ssem, rsem, zsem, zrsem, csem, crsem, xsem, xrsem, lsem):
    nq, _, rows, cw = wg.shape
    tokens = iv.shape[1]
    half = rows // 2
    edge = rxep.shape[1]
    g, me = lax.axis_index("group"), lax.axis_index("fsdp")
    y, x, c = me // 4, lax.rem(me // 2, 2), lax.rem(me, 2)
    z, far = lax.rem(g, NZ), g // NZ
    yp, ym, y2, xo, co = lax.rem(y + 1, 4), lax.rem(y + 3, 4), lax.rem(y + 2, 4), 1 - x, 1 - c
    groups = lax.axis_size("group")

    def at(yy, xx, cc):
        return yy * 4 + xx * 2 + cc

    def chip(yy, xx):
        return yy * 2 + xx

    sib, up, down, side = ((g, at(y, x, co)), (g, at(yp, x, c)), (g, at(ym, x, c)), (g, at(y, xo, c)))

    b0, b1, b2 = lax.rem(z, 2), lax.rem(z // 2, 2), z // 4
    flip0, flip1, flip2, across = ((g + 1 - 2 * b0, me), (g + 2 - 4 * b1, me), (g + 4 - 8 * b2, me), (g + 8 - 16 * far, me))
    partners = [flip0, flip1, flip2, across] if groups > 1 else []
    odd = lax.rem(b0 + b1 + far, 2)
    lower = (1 - b2) * (b0 + b1 + far) + b2 * (1 + 3 * odd)

    neighbours = [sib, up, down, side]
    barrier = pltpu.get_barrier_semaphore()

    def greet(peers):
        for peer in peers:
            pl.semaphore_signal(barrier, inc=1, device_id=peer, device_id_type=MESH)

    greet(neighbours)

    def columns(q):
        return slice(q * cw, (q + 1) * cw)

    def load(src, dst, k):
        copy = pltpu.make_async_copy(src, dst, lsem.at[k])
        copy.start()
        return copy

    l_params = [load(params.at[0, :, columns(q)], pv.at[:, columns(q)], q) for q in range(nq)]
    l_ids = load(ids, iv, nq)

    def block(k, core):
        return act.at[0, :, pl.ds(pl.multiple_of((2 * k + core) * rows, rows), rows)]

    def held(half, k):
        return xk.at[pl.ds(half * tokens, tokens), pl.ds(k * rows, rows)]

    l_act = [load(block(k, c), held(0, k), nq + 8 + k) for k in range(NF // 2)]
    l_tgt = load(tgt.at[0], tv, nq + 2)
    l_anchor = load(anchor, av, nq + 3)
    l_frag = load(fragments, frag, nq + 4)
    l_later = [load(adam_m.at[0], mv, nq + 5), load(adam_v.at[0], vv, nq + 6), load(momentum, uv, nq + 7)]

    sends = {}

    def start(copy, tag=None):
        copy.start()
        sends.setdefault(tag, []).append(copy)

    def settle(tag):
        for copy in sends.pop(tag, []):
            copy.wait_send()

    def settle_gather():
        for q in range(nq):
            settle(-1 - q)

    def remote(src, dst, q, kind, peer):
        return pltpu.make_async_remote_copy(
            src_ref=src, dst_ref=dst, send_sem=ssem.at[q, kind], recv_sem=rsem.at[q, kind],
            device_id=peer, device_id_type=MESH)

    def send(src, dst, q, kind, peer):
        start(remote(src, dst, q, kind, peer), q if kind >= X1 else -1 - q)

    def arrived(dst, q, kind):
        remote(dst, dst, q, kind, sib).wait_recv()

    y1, y3 = y + 1 - 2 * lax.rem(y, 2), 3 - y
    count_peers = [sib, side, (g, at(y1, x, c)), (g, at(y3, x, c))]

    def count_copy(k):
        return pltpu.make_async_remote_copy(
            src_ref=cs.at[k], dst_ref=cr.at[k], send_sem=csem.at[k], recv_sem=crsem.at[k],
            device_id=count_peers[k], device_id_type=MESH)

    def count(k):
        if k == 0:
            l_ids.wait()
            row = jnp.where(iv[...] != 0, 1.0, 0.0).astype(F32)
            live[...] = jnp.transpose(jnp.broadcast_to(row, (HEAD, tokens)))
            part = jnp.broadcast_to(jnp.sum(row), cs.shape[1:])
        else:
            count_copy(k - 1).wait_recv()
            part = cs[k - 1] + cr[k - 1]
        if k < 4:
            cs[k] = part
            start(count_copy(k))
        else:
            total[...] = part

    def zcopy(src, dst, k, peer):
        return pltpu.make_async_remote_copy(
            src_ref=src, dst_ref=dst, send_sem=zsem.at[k], recv_sem=zrsem.at[k],
            device_id=peer, device_id_type=MESH)

    def mean_start():
        l_anchor.wait()
        l_frag.wait()
        diff = av[:, columns(0)] - pv[:, columns(0)]
        for f in range(1, nq):
            diff = jnp.where(jnp.full(diff.shape, frag[0]) == f, av[:, columns(f)] - pv[:, columns(f)], diff)
        dd[...] = diff.reshape(dd.shape)
        if groups > 1:
            @pl.when(lower < 4)
            def _():
                pl.semaphore_wait(barrier, 4 - lower)

            start(zcopy(dd.at[pl.ds(2 - 2 * b0, 2)], from_b, 0, flip0))

    def mean_b():
        if groups > 1:
            zcopy(from_b, from_b, 0, flip0).wait_recv()
            sum_b[...] = dd[pl.ds(2 * b0, 2)] + from_b[...]
            start(zcopy(sum_b.at[1 - b1], from_c, 1, flip1))

    def mean_c():
        if groups > 1:
            zcopy(from_c, from_c, 1, flip1).wait_recv()
            sum_c[...] = sum_b[b1] + from_c[...]
            start(zcopy(sum_c, from_d, 2, across))

    def mean_d():
        if groups > 1:
            zcopy(from_d, from_d, 2, across).wait_recv()
            sum_d[...] = sum_c[...] + from_d[...]
            start(zcopy(sum_d, from_e, 3, flip2))

    mine, other = 2 * b0 + b1, 2 * b0 + 1 - b1

    def mean_e():
        if groups > 1:
            zcopy(from_e, from_e, 3, flip2).wait_recv()
            delta_out[mine] = (sum_d[...] + from_e[...]) / groups
            start(zcopy(delta_out.at[mine], delta_out.at[mine], 4, flip1))

    def mean_f():
        if groups > 1:
            zcopy(delta_out.at[other], delta_out.at[other], 4, flip1).wait_recv()
            half_done = delta_out.at[pl.ds(2 * b0, 2)]
            start(zcopy(half_done, half_done, 5, flip0))

    def mean_end():
        if groups > 1:
            half_done = delta_out.at[pl.ds(2 - 2 * b0, 2)]
            zcopy(half_done, half_done, 5, flip0).wait_recv()
        else:
            delta_out[...] = dd[...]

    def swap(k):
        return pltpu.make_async_remote_copy(
            src_ref=block(k, co), dst_ref=held(1, k), send_sem=xsem.at[k], recv_sem=xrsem.at[k],
            device_id=sib, device_id_type=MESH)

    def swap_start():
        for k in range(NF // 2):
            start(swap(k))

    def swap_end():
        for k in range(NF // 2):
            l_act[k].wait()
            swap(k).wait_recv()

    every, lo, hi = pl.ds(0, rows), pl.ds(0, half), pl.ds(half, half)
    first, but_first = pl.ds(0, edge), pl.ds(edge, rows - edge)
    last, but_last = pl.ds(rows - edge, edge), pl.ds(0, rows - edge)

    def give(q, kind, peer, shard, rng=every):
        ref = wg.at[q, shard, rng]
        send(ref, ref, q, kind, peer)

    def got(q, kind, shard, rng=every):
        arrived(wg.at[q, shard, rng], q, kind)

    def cast(q):
        l_params[q].wait()
        wg[q, chip(y, x)] = pv[:, columns(q)].astype(BF16)

    def own(q):
        if q > 0:
            cast(q)
        shard = chip(y, x)
        give(q, X_OWN, side, shard)
        give(q, YP_OWN, up, shard)
        give(q, YM_OWN, down, shard)

    def from_side(q):
        shard = chip(y, xo)
        got(q, X_OWN, shard)
        give(q, YP_X, up, shard, but_first)
        give(q, YM_X, down, shard, but_last)

    def from_down(q):
        shard = chip(ym, x)
        got(q, YP_OWN, shard)
        give(q, YP_F, up, shard, lo)
        give(q, X_P, side, shard, first)

    def from_up(q):
        shard = chip(yp, x)
        got(q, YM_OWN, shard)
        give(q, YM_F, down, shard, hi)
        give(q, X_M, side, shard, last)

    def far_lo(q):
        shard = chip(y2, x)
        got(q, YP_F, shard, lo)
        give(q, X_FA, side, shard, lo)

    def far_hi(q):
        shard = chip(y2, x)
        got(q, YM_F, shard, hi)
        give(q, X_FB, side, shard, hi)

    def product(q, chips):
        s = None
        for yy, xx in chips:
            k = chip(yy, xx)
            cols = pl.ds(pl.multiple_of(k * rows, rows), rows)
            d = jnp.dot(xk[:, cols], wg[q, k], preferred_element_type=F32)
            s = d if s is None else s + d
        return s

    def keys_a(q):
        acc[q] = product(q, [(y, x), (ym, x), (yp, x), (y, xo)])

    def keys_b(q):
        got(q, YP_X, chip(ym, xo), but_first)
        got(q, X_P, chip(ym, xo), first)
        got(q, YM_X, chip(yp, xo), but_last)
        got(q, X_M, chip(yp, xo), last)
        got(q, X_FA, chip(y2, xo), lo)
        got(q, X_FB, chip(y2, xo), hi)
        s = acc[q] + product(q, [(y2, x), (ym, xo), (yp, xo), (y2, xo)])
        acc[q] = s
        ksend[q] = s[tokens:]
        send(ksend.at[q], krecv.at[q], q, KEYS, sib)

    def residual(q):
        arrived(krecv.at[q], q, KEYS)
        keys = (acc[q, :tokens] + krecv[q]) * scale
        target = tv[:, columns(q)].astype(F32)
        rs[q, :tokens] = (live[...] * (keys - target) / total[0:1, 0:1]).astype(BF16)
        send(rs.at[q, pl.ds(0, tokens)], rs.at[q, pl.ds(tokens, tokens)], q, ROWS, sib)

    def turn(k):
        xt[k] = jnp.transpose(xk[:, k * rows:(k + 1) * rows])

    ready = set()

    def slope(q, yy, xx):
        if q not in ready:
            ready.add(q)
            arrived(rs.at[q, pl.ds(tokens, tokens)], q, ROWS)
        return jnp.dot(xt[chip(yy, xx)], rs[q], preferred_element_type=F32)

    def pass_on(q, buf, dst, rng, value, kind, peer):
        buf[q, rng] = value.astype(BF16)
        send(buf.at[q, rng], dst.at[q, rng], q, kind, peer)

    def sum_cross(q):
        pass_on(q, tx1, rx1, every, slope(q, y2, xo), X1, side)

    def sum_corner_up(q):
        ty1p[q] = slope(q, yp, xo).astype(BF16)
        send(ty1p.at[q, but_first], ry1p.at[q, but_first], q, Y1P, up)
        send(ty1p.at[q, first], rxep.at[q], q, XEP, side)

    def sum_corner_down(q):
        ty1m[q] = slope(q, ym, xo).astype(BF16)
        send(ty1m.at[q, but_last], ry1m.at[q, but_last], q, Y1M, down)
        send(ty1m.at[q, last], rxem.at[q], q, XEM, side)

    def sum_up(q):
        gown[q, 0] = slope(q, yp, x)
        pass_on(q, ty3p, ry3p, hi, gown[q, 0, hi], Y3PB, up)

    def sum_down(q):
        gown[q, 1] = slope(q, ym, x)
        pass_on(q, ty3m, ry3m, lo, gown[q, 1, lo], Y3MA, down)

    def part_far(q):
        gown[q, 2] = slope(q, y2, x)

    def part_side(q):
        gown[q, 3] = slope(q, y, xo)

    def part_own(q):
        gown[q, 4] = slope(q, y, x)

    def sum_far(q):
        arrived(rx1.at[q], q, X1)
        s = gown[q, 2] + rx1[q].astype(F32)
        pass_on(q, ty2p, ry2p, pl.ds(0, half), s[:half], Y2P, up)
        pass_on(q, ty2m, ry2m, pl.ds(0, half), s[half:], Y2M, down)

    def sum_side(q):
        arrived(ry1p.at[q, but_first], q, Y1P)
        arrived(ry1m.at[q, but_last], q, Y1M)
        zero = jnp.zeros((edge, cw), F32)
        s = gown[q, 3] + jnp.concatenate([zero, ry1p[q, but_first].astype(F32)])
        s = s + jnp.concatenate([ry1m[q, but_last].astype(F32), zero])
        pass_on(q, tx2, rx2, every, s, X2, side)

    def sum_up_far(q):
        arrived(ry2p.at[q], q, Y2P)
        arrived(rxep.at[q], q, XEP)
        s = gown[q, 0, lo] + ry2p[q].astype(F32)
        s = s + jnp.concatenate([rxep[q].astype(F32), jnp.zeros((half - edge, cw), F32)])
        pass_on(q, ty3p, ry3p, lo, s, Y3PA, up)

    def sum_down_far(q):
        arrived(ry2m.at[q], q, Y2M)
        arrived(rxem.at[q], q, XEM)
        s = gown[q, 1, hi] + ry2m[q].astype(F32)
        s = s + jnp.concatenate([jnp.zeros((half - edge, cw), F32), rxem[q].astype(F32)])
        pass_on(q, ty3m, ry3m, hi, s, Y3MB, down)

    def finish(q):
        arrived(rx2.at[q], q, X2)
        arrived(ry3p.at[q, hi], q, Y3PB)
        arrived(ry3m.at[q, lo], q, Y3MA)
        arrived(ry3p.at[q, lo], q, Y3PA)
        arrived(ry3m.at[q, hi], q, Y3MB)
        s = gown[q, 4] + rx2[q].astype(F32) + ry3p[q].astype(F32) + ry3m[q].astype(F32)
        grad_out[:, columns(q)] = s * scale

    cast(0)
    pl.semaphore_wait(barrier, len(neighbours) + (lower if groups > 1 else 0))
    greet(partners)
    own(0)
    own(1)
    count(0)
    count(1)
    own(2)
    swap_start()
    swap_end()
    from_up(1)
    count(2)
    turn(5)
    from_down(0)
    from_up(0)
    own(3)
    turn(4)
    mean_start()
    far_lo(0)
    from_up(2)
    from_down(1)
    turn(2)
    far_hi(0)
    from_down(2)
    far_hi(1)
    count(3)
    from_side(0)
    from_side(1)
    from_down(3)
    from_side(2)
    mean_b()
    keys_a(2)
    far_lo(1)
    keys_a(0)
    turn(6)
    from_up(3)
    keys_a(1)
    turn(0)
    count(4)
    far_hi(2)
    far_lo(2)
    turn(3)
    from_side(3)
    turn(7)
    turn(1)
    keys_b(0)
    l_tgt.wait()
    residual(0)
    mean_c()
    keys_b(1)
    sum_cross(0)
    sum_corner_up(0)
    residual(1)
    far_hi(3)
    sum_corner_down(0)
    sum_up(0)
    far_lo(3)
    part_own(0)
    sum_down(1)
    keys_b(2)
    mean_d()
    sum_corner_up(1)
    sum_down(0)
    residual(2)
    sum_cross(1)
    sum_corner_down(1)
    keys_a(3)
    sum_corner_down(2)
    sum_down(2)
    sum_up(1)
    sum_cross(2)
    part_far(1)
    sum_up(2)
    part_side(1)
    part_far(0)
    sum_corner_up(2)
    sum_far(0)
    sum_side(1)
    sum_far(1)
    keys_b(3)
    residual(3)
    part_side(0)
    part_far(2)
    sum_far(2)
    sum_cross(3)
    part_own(3)
    sum_corner_down(3)
    settle_gather()
    part_far(3)
    mean_e()
    sum_corner_up(3)
    part_own(2)
    part_side(3)
    sum_side(0)
    sum_up_far(2)
    sum_down(3)
    sum_up_far(0)
    sum_down_far(1)
    sum_far(3)
    sum_up(3)
    part_side(2)
    sum_up_far(1)
    sum_side(2)
    sum_side(3)
    part_own(1)
    sum_down_far(0)
    mean_f()
    sum_down_far(2)
    sum_down_far(3)
    sum_up_far(3)
    finish(1)
    settle(1)
    finish(0)
    settle(0)
    finish(2)
    settle(2)
    mean_end()
    finish(3)
    for copy in l_later:
        copy.wait()
    for tag in list(sends):
        settle(tag)


def sync(activations, targets, token_ids, sync_fragment, params, adam_m, adam_v, anchor, momentum):
    tokens, width = activations.shape[1:]
    rows, kv = params.shape[1:]
    nq = kv // HEAD
    edge = EDGE * rows // 512
    piece = pltpu.VMEM((nq, rows, HEAD), BF16)
    part = pltpu.VMEM((nq, rows // 2, HEAD), BF16)
    thin = pltpu.VMEM((nq, edge, HEAD), BF16)
    quarter = pltpu.VMEM((rows // 4, HEAD), F32)
    full = jax.ShapeDtypeStruct((rows, kv), F32)
    hbm = pl.BlockSpec(memory_space=pltpu.HBM)
    vmem = pl.BlockSpec(memory_space=pltpu.VMEM)
    return pl.pallas_call(
        functools.partial(sync_kernel, float(width) ** (-0.5)),
        out_shape=(full, jax.ShapeDtypeStruct((4, rows // 4, HEAD), F32)) + (full,) * 5,
        in_specs=[hbm] * 9,
        out_specs=(vmem,) * 7,
        scratch_shapes=[
            pltpu.SMEM(sync_fragment.shape, jnp.int32),
            pltpu.VMEM((2 * tokens, width // 2), BF16),
            pltpu.VMEM((NF // 2, rows, 2 * tokens), BF16),
            pltpu.VMEM((tokens, kv), BF16),
            pltpu.VMEM((1, tokens), jnp.int32),
            pltpu.VMEM((tokens, HEAD), F32),
            pltpu.VMEM((8, HEAD), F32),
            pltpu.VMEM((nq, NF // 2, rows, HEAD), BF16),
            pltpu.VMEM((nq, 2 * tokens, HEAD), F32),
            pltpu.VMEM((nq, tokens, HEAD), F32),
            pltpu.VMEM((nq, tokens, HEAD), F32),
            pltpu.VMEM((nq, 2 * tokens, HEAD), BF16),
            pltpu.VMEM((nq, 5, rows, HEAD), F32),
            piece, piece, piece, thin, thin, part, part, piece, piece, piece,
            piece, piece, piece, part, part, piece, piece, piece,
            pltpu.VMEM((4, rows // 4, HEAD), F32),
            pltpu.VMEM((2, rows // 4, HEAD), F32), quarter, quarter,
            pltpu.VMEM((2, rows // 4, HEAD), F32), quarter, quarter, quarter,
            pltpu.VMEM((4, 8, HEAD), F32),
            pltpu.VMEM((4, 8, HEAD), F32),
            pltpu.SemaphoreType.DMA((nq, KINDS)),
            pltpu.SemaphoreType.DMA((nq, KINDS)),
            pltpu.SemaphoreType.DMA((6,)),
            pltpu.SemaphoreType.DMA((6,)),
            pltpu.SemaphoreType.DMA((4,)),
            pltpu.SemaphoreType.DMA((4,)),
            pltpu.SemaphoreType.DMA((NF // 2,)),
            pltpu.SemaphoreType.DMA((NF // 2,)),
            pltpu.SemaphoreType.DMA((nq + 8 + NF // 2,)),
        ],
        compiler_params=pltpu.CompilerParams(
            collective_id=0, has_side_effects=True, vmem_limit_bytes=36 * 2**20
        ),
        cost_estimate=pl.CostEstimate(
            flops=4 * tokens * width * kv, bytes_accessed=2 * tokens * width + 12 * rows * kv, transcendentals=0
        ),
        name="sync",
    )(*[
        pltpu.with_memory_space_constraint(a, pltpu.HBM)
        for a in (activations, targets, token_ids, sync_fragment, params, adam_m, adam_v, anchor, momentum)
    ])


def update_kernel(steps, frag, grad, delta, params, adam_m, adam_v, anchor, momentum,
                  out_params, out_m, out_v, out_anchor, out_momentum,
                  new_params, new_m, new_v, new_anchor, new_momentum, sem):
    rows = grad.shape[0]
    size = rows // steps
    copies = []

    def store(src, dst):
        copy = pltpu.make_async_copy(src, dst, sem.at[len(copies)])
        copy.start()
        copies.append(copy)

    fragment = pl.ds(pl.multiple_of(frag[0] * HEAD, HEAD), HEAD)
    arriving = pl.ds(pl.multiple_of(frag[1] * HEAD, HEAD), HEAD)
    for i in range(steps):
        r = pl.ds(i * size, size)
        slope = grad[r]
        weight = params[r]
        first = beta_one * adam_m[r] + (1.0 - beta_one) * slope
        second = beta_two * adam_v[r] + (1.0 - beta_two) * slope * slope
        new_m[r] = first
        store(new_m.at[r], out_m.at[0, r])
        new_v[r] = second
        store(new_v.at[r], out_v.at[0, r])
        new_params[r] = weight - learn_rate * (first / (jnp.sqrt(second) + adam_epsilon) + decay_rate * weight)
        new_params[r, arriving] = merge_weight * new_params[r, arriving] + (1.0 - merge_weight) * anchor[r, arriving]
        store(new_params.at[r], out_params.at[0, r])
        new_anchor[r] = anchor[r]
        new_momentum[r] = momentum[r]
        change = delta[r]
        moment = outer_beta * momentum[r, fragment] + change
        new_momentum[r, fragment] = moment
        store(new_momentum.at[r], out_momentum.at[r])
        new_anchor[r, fragment] = anchor[r, fragment] - outer_rate * (change + outer_beta * moment)
        store(new_anchor.at[r], out_anchor.at[r])
    for copy in copies:
        copy.wait()


def update(frag, grad, delta, params, adam_m, adam_v, anchor, momentum, steps=4):
    rows, kv = grad.shape
    vmem = pl.BlockSpec(memory_space=pltpu.VMEM)
    hbm = pl.BlockSpec(memory_space=pltpu.HBM)
    return pl.pallas_call(
        functools.partial(update_kernel, steps),
        out_shape=[jax.ShapeDtypeStruct((1, rows, kv), F32)] * 3 + [jax.ShapeDtypeStruct((rows, kv), F32)] * 2,
        in_specs=[pl.BlockSpec(memory_space=pltpu.SMEM)] + [vmem] * 7,
        out_specs=[hbm] * 5,
        scratch_shapes=[pltpu.VMEM((rows, kv), F32)] * 5 + [pltpu.SemaphoreType.DMA((5 * steps,))],
        compiler_params=pltpu.CompilerParams(vmem_limit_bytes=16 * 2**20),
        name="update",
    )(frag, grad, delta, params, adam_m, adam_v, anchor, momentum)


def on_device(activations, targets, token_ids, sync_fragment, params, adam_m, adam_v, anchor, momentum):
    grad, delta, *held = sync(activations, targets, token_ids, sync_fragment, params, adam_m, adam_v, anchor, momentum)
    delta = delta.reshape(delta.shape[0] * delta.shape[1], delta.shape[2])
    return tuple(update(sync_fragment, grad, delta, *held))


def solution(mesh):
    worker = P("group", "fsdp", None)
    shared = P("fsdp", None)
    return jax.shard_map(
        on_device,
        mesh=mesh,
        in_specs=(worker, worker, P("group", "fsdp"), P(), worker, worker, worker, shared, shared),
        out_specs=(worker, worker, worker, shared, shared),
        check_vma=False,
    )
```

```python
import functools

import jax
import jax.numpy as jnp
from jax import lax
from jax.experimental import pallas as pl
from jax.experimental.pallas import tpu as pltpu
from jax.sharding import PartitionSpec as P

HEAD = 128
MESH = pl.DeviceIdType.MESH
F32 = jnp.float32
BF16 = jnp.bfloat16

beta_one = 0.9
beta_two = 0.999
learn_rate = 0.05
decay_rate = 0.1
adam_epsilon = 1e-08
outer_rate = 0.7
outer_beta = 0.9
merge_weight = 0.5

NF = 16
NZ = 8

EDGE = 80

(X_OWN, YP_OWN, YM_OWN, YP_X, YM_X, YP_F, YM_F, X_P, X_M, X_FA, X_FB, KEYS, ROWS,
 X1, Y1P, Y1M, XEP, XEM, Y2P, Y2M, Y3PB, Y3PA, Y3MA, Y3MB, X2) = range(25)
KINDS = 25


def sync_kernel(scale, act, tgt, ids, fragments, params, adam_m, adam_v, anchor, momentum,
                grad_out, delta_out, pv, mv, vv, av, uv,
                frag, xk, xt, tv, iv, live, total, wg, acc, ksend, krecv, rs, gown,
                rx1, ry1p, ry1m, rxep, rxem, ry2p, ry2m, ry3p, ry3m, rx2,
                tx1, ty1p, ty1m, ty2p, ty2m, ty3p, ty3m, tx2,
                dd, sum_b, sum_c, from_b, from_c, from_d, from_upper, cs, cr,
                ssem, rsem, zsem, zrsem, csem, crsem, xsem, xrsem, lsem):
    nq, _, rows, cw = wg.shape
    tokens = iv.shape[1]
    half = rows // 2
    edge = rxep.shape[1]
    g, me = lax.axis_index("group"), lax.axis_index("fsdp")
    y, x, c = me // 4, lax.rem(me // 2, 2), lax.rem(me, 2)
    z, far = lax.rem(g, NZ), g // NZ
    yp, ym, y2, xo, co = lax.rem(y + 1, 4), lax.rem(y + 3, 4), lax.rem(y + 2, 4), 1 - x, 1 - c
    groups = lax.axis_size("group")

    def at(yy, xx, cc):
        return yy * 4 + xx * 2 + cc

    def chip(yy, xx):
        return yy * 2 + xx

    sib, up, down, side = ((g, at(y, x, co)), (g, at(yp, x, c)), (g, at(ym, x, c)), (g, at(y, xo, c)))

    b0, b1, upper = lax.rem(z, 2), lax.rem(z // 2, 2), z // 4
    mine, other = 2 * b0 + b1, 2 * b0 + 1 - b1
    flip0, flip1, across = (g + 1 - 2 * b0, me), (g + 2 - 4 * b1, me), (g + 8 - 16 * far, me)
    before = b0 + b1 + far

    def holder(k):
        return (far * NZ + k // 2 + 2 * (k % 2), me)

    def hearer(k):
        return (far * NZ + 4 + k // 2 + 2 * (k % 2), me)

    grouped = groups > 1
    is_lower, is_upper = upper == 0, upper == 1

    neighbours = [sib, up, down, side]
    barrier = pltpu.get_barrier_semaphore()

    def greet(peers):
        for peer in peers:
            pl.semaphore_signal(barrier, inc=1, device_id=peer, device_id_type=MESH)

    greet(neighbours)

    def columns(q):
        return slice(q * cw, (q + 1) * cw)

    def load(src, dst, k):
        copy = pltpu.make_async_copy(src, dst, lsem.at[k])
        copy.start()
        return copy

    l_params = [load(params.at[0, :, columns(q)], pv.at[:, columns(q)], q) for q in range(nq)]
    l_ids = load(ids, iv, nq)

    def block(k, core):
        return act.at[0, :, pl.ds(pl.multiple_of((2 * k + core) * rows, rows), rows)]

    def held(half, k):
        return xk.at[pl.ds(half * tokens, tokens), pl.ds(k * rows, rows)]

    l_act = [load(block(k, c), held(0, k), nq + 8 + k) for k in range(NF // 2)]
    l_tgt = load(tgt.at[0], tv, nq + 2)
    l_anchor = load(anchor, av, nq + 3)
    l_frag = load(fragments, frag, nq + 4)
    l_later = [load(adam_m.at[0], mv, nq + 5), load(adam_v.at[0], vv, nq + 6), load(momentum, uv, nq + 7)]

    sends = {}

    def start(copy, tag=None):
        copy.start()
        sends.setdefault(tag, []).append(copy)

    def settle(tag):
        for copy in sends.pop(tag, []):
            copy.wait_send()

    def settle_gather():
        for q in range(nq):
            settle(-1 - q)

    def remote(src, dst, q, kind, peer):
        return pltpu.make_async_remote_copy(
            src_ref=src, dst_ref=dst, send_sem=ssem.at[q, kind], recv_sem=rsem.at[q, kind],
            device_id=peer, device_id_type=MESH)

    def send(src, dst, q, kind, peer):
        start(remote(src, dst, q, kind, peer), q if kind >= X1 else -1 - q)

    def arrived(dst, q, kind):
        remote(dst, dst, q, kind, sib).wait_recv()

    y1, y3 = y + 1 - 2 * lax.rem(y, 2), 3 - y
    count_peers = [sib, side, (g, at(y1, x, c)), (g, at(y3, x, c))]

    def count_copy(k):
        return pltpu.make_async_remote_copy(
            src_ref=cs.at[k], dst_ref=cr.at[k], send_sem=csem.at[k], recv_sem=crsem.at[k],
            device_id=count_peers[k], device_id_type=MESH)

    def count(k):
        if k == 0:
            l_ids.wait()
            row = jnp.where(iv[...] != 0, 1.0, 0.0).astype(F32)
            live[...] = jnp.transpose(jnp.broadcast_to(row, (HEAD, tokens)))
            part = jnp.broadcast_to(jnp.sum(row), cs.shape[1:])
        else:
            count_copy(k - 1).wait_recv()
            part = cs[k - 1] + cr[k - 1]
        if k < 4:
            cs[k] = part
            start(count_copy(k))
        else:
            total[...] = part

    def zcopy(src, dst, k, peer):
        return pltpu.make_async_remote_copy(
            src_ref=src, dst_ref=dst, send_sem=zsem.at[k], recv_sem=zrsem.at[k],
            device_id=peer, device_id_type=MESH)

    def to_holder(k):
        return pltpu.make_async_remote_copy(
            src_ref=dd.at[k], dst_ref=from_upper.at[mine], send_sem=zsem.at[6 + k], recv_sem=zrsem.at[6 + mine],
            device_id=holder(k), device_id_type=MESH)

    def to_hearer(k):
        return pltpu.make_async_remote_copy(
            src_ref=delta_out.at[mine], dst_ref=delta_out.at[mine], send_sem=zsem.at[10 + k], recv_sem=zrsem.at[10 + mine],
            device_id=hearer(k), device_id_type=MESH)

    def mean_start():
        l_anchor.wait()
        l_frag.wait()
        diff = av[:, columns(0)] - pv[:, columns(0)]
        for f in range(1, nq):
            diff = jnp.where(jnp.full(diff.shape, frag[0]) == f, av[:, columns(f)] - pv[:, columns(f)], diff)
        dd[...] = diff.reshape(dd.shape)
        if grouped:
            @pl.when(is_upper)
            def _():
                for k in range(4):
                    to_holder(k).start()

    def mean_a():
        if grouped:
            @pl.when(is_lower)
            def _():
                pl.semaphore_wait(barrier, 7 - before)
                zcopy(dd.at[pl.ds(2 - 2 * b0, 2)], from_b, 0, flip0).start()

    def mean_b():
        if grouped:
            @pl.when(is_lower)
            def _():
                zcopy(from_b, from_b, 0, flip0).wait_recv()
                sum_b[...] = dd[pl.ds(2 * b0, 2)] + from_b[...]
                zcopy(sum_b.at[1 - b1], from_c, 1, flip1).start()

    def mean_c():
        if grouped:
            @pl.when(is_lower)
            def _():
                zcopy(from_c, from_c, 1, flip1).wait_recv()
                s = sum_b[b1] + from_c[...]
                for k in range(4):
                    slot = from_upper.at[k]
                    zcopy(slot, slot, 6 + k, flip1).wait_recv()
                    s = s + from_upper[k]
                sum_c[...] = s
                zcopy(sum_c, from_d, 2, across).start()

    def mean_d():
        if grouped:
            @pl.when(is_lower)
            def _():
                zcopy(from_d, from_d, 2, across).wait_recv()
                delta_out[mine] = (sum_c[...] + from_d[...]) / groups
                zcopy(delta_out.at[mine], delta_out.at[mine], 4, flip1).start()
                for k in range(4):
                    to_hearer(k).start()

    def mean_e():
        if grouped:
            @pl.when(is_lower)
            def _():
                zcopy(delta_out.at[other], delta_out.at[other], 4, flip1).wait_recv()
                half_done = delta_out.at[pl.ds(2 * b0, 2)]
                zcopy(half_done, half_done, 5, flip0).start()

    def mean_end():
        if grouped:
            @pl.when(is_lower)
            def _():
                half_done = delta_out.at[pl.ds(2 - 2 * b0, 2)]
                zcopy(half_done, half_done, 5, flip0).wait_recv()
                for copy in (zcopy(from_b, from_b, 0, flip0), zcopy(from_c, from_c, 1, flip1), zcopy(sum_c, from_d, 2, across),
                             zcopy(sum_c, from_d, 4, flip1), zcopy(half_done, half_done, 5, flip0)):
                    copy.wait_send()
                for k in range(4):
                    to_hearer(k).wait_send()

            @pl.when(is_upper)
            def _():
                for k in range(4):
                    slot = delta_out.at[k]
                    zcopy(slot, slot, 10 + k, flip1).wait_recv()
                for k in range(4):
                    to_holder(k).wait_send()
        else:
            delta_out[...] = dd[...]

    def swap(k):
        return pltpu.make_async_remote_copy(
            src_ref=block(k, co), dst_ref=held(1, k), send_sem=xsem.at[k], recv_sem=xrsem.at[k],
            device_id=sib, device_id_type=MESH)

    def swap_start():
        for k in range(NF // 2):
            start(swap(k))

    def swap_end():
        for k in range(NF // 2):
            l_act[k].wait()
            swap(k).wait_recv()

    every, lo, hi = pl.ds(0, rows), pl.ds(0, half), pl.ds(half, half)
    first, but_first = pl.ds(0, edge), pl.ds(edge, rows - edge)
    last, but_last = pl.ds(rows - edge, edge), pl.ds(0, rows - edge)

    def give(q, kind, peer, shard, rng=every):
        ref = wg.at[q, shard, rng]
        send(ref, ref, q, kind, peer)

    def got(q, kind, shard, rng=every):
        arrived(wg.at[q, shard, rng], q, kind)

    def cast(q):
        l_params[q].wait()
        wg[q, chip(y, x)] = pv[:, columns(q)].astype(BF16)

    def own(q):
        if q > 0:
            cast(q)
        shard = chip(y, x)
        give(q, X_OWN, side, shard)
        give(q, YP_OWN, up, shard)
        give(q, YM_OWN, down, shard)

    def from_side(q):
        shard = chip(y, xo)
        got(q, X_OWN, shard)
        give(q, YP_X, up, shard, but_first)
        give(q, YM_X, down, shard, but_last)

    def from_down(q):
        shard = chip(ym, x)
        got(q, YP_OWN, shard)
        give(q, YP_F, up, shard, lo)
        give(q, X_P, side, shard, first)

    def from_up(q):
        shard = chip(yp, x)
        got(q, YM_OWN, shard)
        give(q, YM_F, down, shard, hi)
        give(q, X_M, side, shard, last)

    def far_lo(q):
        shard = chip(y2, x)
        got(q, YP_F, shard, lo)
        give(q, X_FA, side, shard, lo)

    def far_hi(q):
        shard = chip(y2, x)
        got(q, YM_F, shard, hi)
        give(q, X_FB, side, shard, hi)

    def product(q, chips):
        s = None
        for yy, xx in chips:
            k = chip(yy, xx)
            cols = pl.ds(pl.multiple_of(k * rows, rows), rows)
            d = jnp.dot(xk[:, cols], wg[q, k], preferred_element_type=F32)
            s = d if s is None else s + d
        return s

    def keys_a(q):
        acc[q] = product(q, [(y, x), (ym, x), (yp, x), (y, xo)])

    def keys_b(q):
        got(q, YP_X, chip(ym, xo), but_first)
        got(q, X_P, chip(ym, xo), first)
        got(q, YM_X, chip(yp, xo), but_last)
        got(q, X_M, chip(yp, xo), last)
        got(q, X_FA, chip(y2, xo), lo)
        got(q, X_FB, chip(y2, xo), hi)
        s = acc[q] + product(q, [(y2, x), (ym, xo), (yp, xo), (y2, xo)])
        acc[q] = s
        ksend[q] = s[tokens:]
        send(ksend.at[q], krecv.at[q], q, KEYS, sib)

    def residual(q):
        arrived(krecv.at[q], q, KEYS)
        keys = (acc[q, :tokens] + krecv[q]) * scale
        target = tv[:, columns(q)].astype(F32)
        rs[q, :tokens] = (live[...] * (keys - target) / total[0:1, 0:1]).astype(BF16)
        send(rs.at[q, pl.ds(0, tokens)], rs.at[q, pl.ds(tokens, tokens)], q, ROWS, sib)

    def turn(k):
        xt[k] = jnp.transpose(xk[:, k * rows:(k + 1) * rows])

    ready = set()

    def slope(q, yy, xx):
        if q not in ready:
            ready.add(q)
            arrived(rs.at[q, pl.ds(tokens, tokens)], q, ROWS)
        return jnp.dot(xt[chip(yy, xx)], rs[q], preferred_element_type=F32)

    def pass_on(q, buf, dst, rng, value, kind, peer):
        buf[q, rng] = value.astype(BF16)
        send(buf.at[q, rng], dst.at[q, rng], q, kind, peer)

    def sum_cross(q):
        pass_on(q, tx1, rx1, every, slope(q, y2, xo), X1, side)

    def sum_corner_up(q):
        ty1p[q] = slope(q, yp, xo).astype(BF16)
        send(ty1p.at[q, but_first], ry1p.at[q, but_first], q, Y1P, up)
        send(ty1p.at[q, first], rxep.at[q], q, XEP, side)

    def sum_corner_down(q):
        ty1m[q] = slope(q, ym, xo).astype(BF16)
        send(ty1m.at[q, but_last], ry1m.at[q, but_last], q, Y1M, down)
        send(ty1m.at[q, last], rxem.at[q], q, XEM, side)

    def sum_up(q):
        gown[q, 0] = slope(q, yp, x)
        pass_on(q, ty3p, ry3p, hi, gown[q, 0, hi], Y3PB, up)

    def sum_down(q):
        gown[q, 1] = slope(q, ym, x)
        pass_on(q, ty3m, ry3m, lo, gown[q, 1, lo], Y3MA, down)

    def part_far(q):
        gown[q, 2] = slope(q, y2, x)

    def part_side(q):
        gown[q, 3] = slope(q, y, xo)

    def part_own(q):
        gown[q, 4] = slope(q, y, x)

    def sum_far(q):
        arrived(rx1.at[q], q, X1)
        s = gown[q, 2] + rx1[q].astype(F32)
        pass_on(q, ty2p, ry2p, pl.ds(0, half), s[:half], Y2P, up)
        pass_on(q, ty2m, ry2m, pl.ds(0, half), s[half:], Y2M, down)

    def sum_side(q):
        arrived(ry1p.at[q, but_first], q, Y1P)
        arrived(ry1m.at[q, but_last], q, Y1M)
        zero = jnp.zeros((edge, cw), F32)
        s = gown[q, 3] + jnp.concatenate([zero, ry1p[q, but_first].astype(F32)])
        s = s + jnp.concatenate([ry1m[q, but_last].astype(F32), zero])
        pass_on(q, tx2, rx2, every, s, X2, side)

    def sum_up_far(q):
        arrived(ry2p.at[q], q, Y2P)
        arrived(rxep.at[q], q, XEP)
        s = gown[q, 0, lo] + ry2p[q].astype(F32)
        s = s + jnp.concatenate([rxep[q].astype(F32), jnp.zeros((half - edge, cw), F32)])
        pass_on(q, ty3p, ry3p, lo, s, Y3PA, up)

    def sum_down_far(q):
        arrived(ry2m.at[q], q, Y2M)
        arrived(rxem.at[q], q, XEM)
        s = gown[q, 1, hi] + ry2m[q].astype(F32)
        s = s + jnp.concatenate([jnp.zeros((half - edge, cw), F32), rxem[q].astype(F32)])
        pass_on(q, ty3m, ry3m, hi, s, Y3MB, down)

    def finish(q):
        arrived(rx2.at[q], q, X2)
        arrived(ry3p.at[q, hi], q, Y3PB)
        arrived(ry3m.at[q, lo], q, Y3MA)
        arrived(ry3p.at[q, lo], q, Y3PA)
        arrived(ry3m.at[q, hi], q, Y3MB)
        s = gown[q, 4] + rx2[q].astype(F32) + ry3p[q].astype(F32) + ry3m[q].astype(F32)
        grad_out[:, columns(q)] = s * scale

    cast(0)
    if grouped:
        pl.semaphore_wait(barrier, len(neighbours) + (1 - upper) * before + upper * 4)

        @pl.when(is_lower)
        def _():
            greet([flip0, flip1, across] + [hearer(k) for k in range(4)])

        @pl.when(is_upper)
        def _():
            greet([holder(k) for k in range(4)])
    else:
        pl.semaphore_wait(barrier, len(neighbours))
    own(0)
    swap_start()
    own(2)
    own(1)
    own(3)
    mean_start()
    swap_end()
    count(0)
    count(1)
    turn(7)
    from_up(0)
    turn(2)
    turn(1)
    mean_a()
    from_down(0)
    from_up(1)
    turn(3)
    turn(5)
    from_down(1)
    turn(0)
    from_up(2)
    turn(6)
    turn(4)
    count(2)
    from_down(3)
    from_side(0)
    far_lo(0)
    from_side(1)
    far_hi(0)
    mean_b()
    keys_a(0)
    far_lo(1)
    far_hi(1)
    count(3)
    from_up(3)
    from_down(2)
    keys_a(1)
    far_hi(2)
    from_side(2)
    keys_a(2)
    keys_b(0)
    from_side(3)
    mean_c()
    keys_b(1)
    far_lo(3)
    count(4)
    l_tgt.wait()
    residual(0)
    far_lo(2)
    keys_a(3)
    far_hi(3)
    residual(1)
    sum_cross(0)
    sum_corner_up(0)
    sum_corner_down(0)
    sum_up(0)
    sum_corner_up(1)
    sum_down(0)
    keys_b(2)
    sum_corner_down(1)
    keys_b(3)
    sum_cross(1)
    residual(2)
    part_far(0)
    sum_far(0)
    mean_d()
    residual(3)
    sum_corner_up(2)
    sum_corner_down(2)
    sum_cross(2)
    part_far(1)
    sum_corner_down(3)
    settle_gather()
    sum_corner_up(3)
    sum_down_far(0)
    sum_down(2)
    sum_cross(3)
    sum_up_far(0)
    part_side(1)
    part_side(0)
    sum_far(1)
    part_far(2)
    sum_down(1)
    part_side(3)
    part_far(3)
    part_side(2)
    sum_side(0)
    sum_side(1)
    sum_far(2)
    sum_side(3)
    sum_far(3)
    sum_side(2)
    sum_up(2)
    sum_up(3)
    sum_up(1)
    sum_up_far(1)
    mean_e()
    part_own(1)
    sum_down(3)
    sum_down_far(1)
    part_own(0)
    part_own(2)
    sum_down_far(3)
    sum_up_far(3)
    part_own(3)
    sum_down_far(2)
    sum_up_far(2)
    finish(0)
    settle(0)
    finish(1)
    settle(1)
    finish(3)
    settle(3)
    mean_end()
    finish(2)
    for copy in l_later:
        copy.wait()
    for tag in list(sends):
        settle(tag)


def sync(activations, targets, token_ids, sync_fragment, params, adam_m, adam_v, anchor, momentum):
    tokens, width = activations.shape[1:]
    rows, kv = params.shape[1:]
    nq = kv // HEAD
    edge = EDGE * rows // 512
    piece = pltpu.VMEM((nq, rows, HEAD), BF16)
    part = pltpu.VMEM((nq, rows // 2, HEAD), BF16)
    thin = pltpu.VMEM((nq, edge, HEAD), BF16)
    quarter = pltpu.VMEM((rows // 4, HEAD), F32)
    full = jax.ShapeDtypeStruct((rows, kv), F32)
    hbm = pl.BlockSpec(memory_space=pltpu.HBM)
    vmem = pl.BlockSpec(memory_space=pltpu.VMEM)
    return pl.pallas_call(
        functools.partial(sync_kernel, float(width) ** (-0.5)),
        out_shape=(full, jax.ShapeDtypeStruct((4, rows // 4, HEAD), F32)) + (full,) * 5,
        in_specs=[hbm] * 9,
        out_specs=(vmem,) * 7,
        scratch_shapes=[
            pltpu.SMEM(sync_fragment.shape, jnp.int32),
            pltpu.VMEM((2 * tokens, width // 2), BF16),
            pltpu.VMEM((NF // 2, rows, 2 * tokens), BF16),
            pltpu.VMEM((tokens, kv), BF16),
            pltpu.VMEM((1, tokens), jnp.int32),
            pltpu.VMEM((tokens, HEAD), F32),
            pltpu.VMEM((8, HEAD), F32),
            pltpu.VMEM((nq, NF // 2, rows, HEAD), BF16),
            pltpu.VMEM((nq, 2 * tokens, HEAD), F32),
            pltpu.VMEM((nq, tokens, HEAD), F32),
            pltpu.VMEM((nq, tokens, HEAD), F32),
            pltpu.VMEM((nq, 2 * tokens, HEAD), BF16),
            pltpu.VMEM((nq, 5, rows, HEAD), F32),
            piece, piece, piece, thin, thin, part, part, piece, piece, piece,
            piece, piece, piece, part, part, piece, piece, piece,
            pltpu.VMEM((4, rows // 4, HEAD), F32),
            pltpu.VMEM((2, rows // 4, HEAD), F32), quarter,
            pltpu.VMEM((2, rows // 4, HEAD), F32), quarter, quarter,
            pltpu.VMEM((4, rows // 4, HEAD), F32),
            pltpu.VMEM((4, 8, HEAD), F32),
            pltpu.VMEM((4, 8, HEAD), F32),
            pltpu.SemaphoreType.DMA((nq, KINDS)),
            pltpu.SemaphoreType.DMA((nq, KINDS)),
            pltpu.SemaphoreType.DMA((14,)),
            pltpu.SemaphoreType.DMA((14,)),
            pltpu.SemaphoreType.DMA((4,)),
            pltpu.SemaphoreType.DMA((4,)),
            pltpu.SemaphoreType.DMA((NF // 2,)),
            pltpu.SemaphoreType.DMA((NF // 2,)),
            pltpu.SemaphoreType.DMA((nq + 8 + NF // 2,)),
        ],
        compiler_params=pltpu.CompilerParams(
            collective_id=0, has_side_effects=True, vmem_limit_bytes=36 * 2**20
        ),
        cost_estimate=pl.CostEstimate(
            flops=4 * tokens * width * kv, bytes_accessed=2 * tokens * width + 12 * rows * kv, transcendentals=0
        ),
        name="sync",
    )(*[
        pltpu.with_memory_space_constraint(a, pltpu.HBM)
        for a in (activations, targets, token_ids, sync_fragment, params, adam_m, adam_v, anchor, momentum)
    ])


def update_kernel(steps, frag, grad, delta, params, adam_m, adam_v, anchor, momentum,
                  out_params, out_m, out_v, out_anchor, out_momentum,
                  new_params, new_m, new_v, new_anchor, new_momentum, sem):
    rows = grad.shape[0]
    size = rows // steps
    copies = []

    def store(src, dst):
        copy = pltpu.make_async_copy(src, dst, sem.at[len(copies)])
        copy.start()
        copies.append(copy)

    fragment = pl.ds(pl.multiple_of(frag[0] * HEAD, HEAD), HEAD)
    arriving = pl.ds(pl.multiple_of(frag[1] * HEAD, HEAD), HEAD)
    for i in range(steps):
        r = pl.ds(i * size, size)
        slope = grad[r]
        weight = params[r]
        first = beta_one * adam_m[r] + (1.0 - beta_one) * slope
        second = beta_two * adam_v[r] + (1.0 - beta_two) * slope * slope
        new_m[r] = first
        store(new_m.at[r], out_m.at[0, r])
        new_v[r] = second
        store(new_v.at[r], out_v.at[0, r])
        new_params[r] = weight - learn_rate * (first / (jnp.sqrt(second) + adam_epsilon) + decay_rate * weight)
        new_params[r, arriving] = merge_weight * new_params[r, arriving] + (1.0 - merge_weight) * anchor[r, arriving]
        store(new_params.at[r], out_params.at[0, r])
        new_anchor[r] = anchor[r]
        new_momentum[r] = momentum[r]
        change = delta[r]
        moment = outer_beta * momentum[r, fragment] + change
        new_momentum[r, fragment] = moment
        store(new_momentum.at[r], out_momentum.at[r])
        new_anchor[r, fragment] = anchor[r, fragment] - outer_rate * (change + outer_beta * moment)
        store(new_anchor.at[r], out_anchor.at[r])
    for copy in copies:
        copy.wait()


def update(frag, grad, delta, params, adam_m, adam_v, anchor, momentum, steps=4):
    rows, kv = grad.shape
    vmem = pl.BlockSpec(memory_space=pltpu.VMEM)
    hbm = pl.BlockSpec(memory_space=pltpu.HBM)
    return pl.pallas_call(
        functools.partial(update_kernel, steps),
        out_shape=[jax.ShapeDtypeStruct((1, rows, kv), F32)] * 3 + [jax.ShapeDtypeStruct((rows, kv), F32)] * 2,
        in_specs=[pl.BlockSpec(memory_space=pltpu.SMEM)] + [vmem] * 7,
        out_specs=[hbm] * 5,
        scratch_shapes=[pltpu.VMEM((rows, kv), F32)] * 5 + [pltpu.SemaphoreType.DMA((5 * steps,))],
        compiler_params=pltpu.CompilerParams(vmem_limit_bytes=16 * 2**20),
        name="update",
    )(frag, grad, delta, params, adam_m, adam_v, anchor, momentum)


def on_device(activations, targets, token_ids, sync_fragment, params, adam_m, adam_v, anchor, momentum):
    grad, delta, *held = sync(activations, targets, token_ids, sync_fragment, params, adam_m, adam_v, anchor, momentum)
    delta = delta.reshape(delta.shape[0] * delta.shape[1], delta.shape[2])
    return tuple(update(sync_fragment, grad, delta, *held))


def solution(mesh):
    worker = P("group", "fsdp", None)
    shared = P("fsdp", None)
    return jax.shard_map(
        on_device,
        mesh=mesh,
        in_specs=(worker, worker, P("group", "fsdp"), P(), worker, worker, worker, shared, shared),
        out_specs=(worker, worker, worker, shared, shared),
        check_vma=False,
    )
```

```python
import functools

import jax
import jax.numpy as jnp
from jax import lax
from jax.experimental import pallas as pl
from jax.experimental.pallas import tpu as pltpu
from jax.sharding import PartitionSpec as P

HEAD = 128
MESH = pl.DeviceIdType.MESH
F32 = jnp.float32
BF16 = jnp.bfloat16

beta_one = 0.9
beta_two = 0.999
learn_rate = 0.05
decay_rate = 0.1
adam_epsilon = 1e-08
outer_rate = 0.7
outer_beta = 0.9
merge_weight = 0.5

NF = 16
NZ = 8

EDGE = 80

(X_OWN, YP_OWN, YM_OWN, YP_X, YM_X, YP_F, YM_F, X_P, X_M, X_FA, X_FB, KEYS, ROWS,
 X1, Y1P, Y1M, XEP, XEM, Y2P, Y2M, Y3PB, Y3PA, Y3MA, Y3MB, X2) = range(25)
KINDS = 25


def sync_kernel(scale, act, tgt, ids, fragments, params, adam_m, adam_v, anchor, momentum,
                grad_out, delta_out, pv, mv, vv, av, uv,
                frag, xk, xt, tv, iv, live, total, wg, acc, ksend, krecv, rs, gown,
                rx1, ry1p, ry1m, rxep, rxem, ry2p, ry2m, ry3p, ry3m, rx2,
                tx1, ty1p, ty1m, ty2p, ty2m, ty3p, ty3m, tx2,
                dd, sum_b, sum_c, from_b, from_c, from_near, from_far, total_c, from_upper, cs, cr,
                ssem, rsem, zsem, zrsem, csem, crsem, xsem, xrsem, lsem):
    nq, _, rows, cw = wg.shape
    tokens = iv.shape[1]
    half = rows // 2
    edge = rxep.shape[1]
    g, me = lax.axis_index("group"), lax.axis_index("fsdp")
    y, x, c = me // 4, lax.rem(me // 2, 2), lax.rem(me, 2)
    z, far = lax.rem(g, NZ), g // NZ
    yp, ym, y2, xo, co = lax.rem(y + 1, 4), lax.rem(y + 3, 4), lax.rem(y + 2, 4), 1 - x, 1 - c
    groups = lax.axis_size("group")

    def at(yy, xx, cc):
        return yy * 4 + xx * 2 + cc

    def chip(yy, xx):
        return yy * 2 + xx

    sib, up, down, side = ((g, at(y, x, co)), (g, at(yp, x, c)), (g, at(ym, x, c)), (g, at(y, xo, c)))

    b0, b1, upper = lax.rem(z, 2), lax.rem(z // 2, 2), z // 4
    mine, other = 2 * b0 + b1, 2 * b0 + 1 - b1
    flip0, flip1 = (g + 1 - 2 * b0, me), (g + 2 - 4 * b1, me)
    facing = (1 - upper) * 4 + 2 * (1 - b1)
    mate, opposite = (far * NZ + facing + b0, me), ((1 - far) * NZ + facing + b0, me)
    before = b0 + b1

    def faced(k):
        return (far * NZ + facing + k, me)

    grouped = groups > 1
    is_lower, is_upper = upper == 0, upper == 1
    adds = upper * far == 1

    neighbours = [sib, up, down, side]
    barrier = pltpu.get_barrier_semaphore()

    def greet(peers):
        for peer in peers:
            pl.semaphore_signal(barrier, inc=1, device_id=peer, device_id_type=MESH)

    greet(neighbours)

    def columns(q):
        return slice(q * cw, (q + 1) * cw)

    def load(src, dst, k):
        copy = pltpu.make_async_copy(src, dst, lsem.at[k])
        copy.start()
        return copy

    l_params = [load(params.at[0, :, columns(q)], pv.at[:, columns(q)], q) for q in range(nq)]
    l_ids = load(ids, iv, nq)

    def block(k, core):
        return act.at[0, :, pl.ds(pl.multiple_of((2 * k + core) * rows, rows), rows)]

    def held(half, k):
        return xk.at[pl.ds(half * tokens, tokens), pl.ds(k * rows, rows)]

    l_act = [load(block(k, c), held(0, k), nq + 8 + k) for k in range(NF // 2)]
    l_tgt = load(tgt.at[0], tv, nq + 2)
    l_anchor = load(anchor, av, nq + 3)
    l_frag = load(fragments, frag, nq + 4)
    l_later = [load(adam_m.at[0], mv, nq + 5), load(adam_v.at[0], vv, nq + 6), load(momentum, uv, nq + 7)]

    sends = {}

    def start(copy, tag=None):
        copy.start()
        sends.setdefault(tag, []).append(copy)

    def settle(tag):
        for copy in sends.pop(tag, []):
            copy.wait_send()

    def settle_gather():
        for q in range(nq):
            settle(-1 - q)

    def remote(src, dst, q, kind, peer):
        return pltpu.make_async_remote_copy(
            src_ref=src, dst_ref=dst, send_sem=ssem.at[q, kind], recv_sem=rsem.at[q, kind],
            device_id=peer, device_id_type=MESH)

    def send(src, dst, q, kind, peer):
        start(remote(src, dst, q, kind, peer), q if kind >= X1 else -1 - q)

    def arrived(dst, q, kind):
        remote(dst, dst, q, kind, sib).wait_recv()

    y1, y3 = y + 1 - 2 * lax.rem(y, 2), 3 - y
    count_peers = [sib, side, (g, at(y1, x, c)), (g, at(y3, x, c))]

    def count_copy(k):
        return pltpu.make_async_remote_copy(
            src_ref=cs.at[k], dst_ref=cr.at[k], send_sem=csem.at[k], recv_sem=crsem.at[k],
            device_id=count_peers[k], device_id_type=MESH)

    def count(k):
        if k == 0:
            l_ids.wait()
            row = jnp.where(iv[...] != 0, 1.0, 0.0).astype(F32)
            live[...] = jnp.transpose(jnp.broadcast_to(row, (HEAD, tokens)))
            part = jnp.broadcast_to(jnp.sum(row), cs.shape[1:])
        else:
            count_copy(k - 1).wait_recv()
            part = cs[k - 1] + cr[k - 1]
        if k < 4:
            cs[k] = part
            start(count_copy(k))
        else:
            total[...] = part

    def zcopy(src, dst, k, peer):
        return pltpu.make_async_remote_copy(
            src_ref=src, dst_ref=dst, send_sem=zsem.at[k], recv_sem=zrsem.at[k],
            device_id=peer, device_id_type=MESH)

    def to_holder(k):
        return pltpu.make_async_remote_copy(
            src_ref=dd.at[pl.ds(2 * k, 2)], dst_ref=from_upper.at[b0], send_sem=zsem.at[6 + k], recv_sem=zrsem.at[6 + b0],
            device_id=faced(k), device_id_type=MESH)

    def to_hearer(k, quarter, i):
        return pltpu.make_async_remote_copy(
            src_ref=delta_out.at[quarter], dst_ref=delta_out.at[quarter], send_sem=zsem.at[8 + i], recv_sem=zrsem.at[10 + quarter],
            device_id=faced(k), device_id_type=MESH)

    def mean_start():
        l_anchor.wait()
        l_frag.wait()
        diff = av[:, columns(0)] - pv[:, columns(0)]
        for f in range(1, nq):
            diff = jnp.where(jnp.full(diff.shape, frag[0]) == f, av[:, columns(f)] - pv[:, columns(f)], diff)
        dd[...] = diff.reshape(dd.shape)
        if grouped:
            @pl.when(is_upper)
            def _():
                for k in range(2):
                    to_holder(k).start()

    def mean_a():
        if grouped:
            @pl.when(is_lower)
            def _():
                pl.semaphore_wait(barrier, 5 - before - far)
                zcopy(dd.at[pl.ds(2 - 2 * b0, 2)], from_b, 0, flip0).start()

    def mean_b():
        if grouped:
            @pl.when(is_lower)
            def _():
                zcopy(from_b, from_b, 0, flip0).wait_recv()
                s = dd[pl.ds(2 * b0, 2)] + from_b[...]
                for k in range(2):
                    zcopy(from_upper.at[k], from_upper.at[k], 6 + k, flip0).wait_recv()
                    s = s + from_upper[k]
                sum_b[...] = s
                zcopy(sum_b.at[1 - b1], from_c, 1, flip1).start()

    def mean_c():
        if grouped:
            @pl.when(is_lower)
            def _():
                zcopy(from_c, from_c, 1, flip1).wait_recv()
                sum_c[...] = sum_b[b1] + from_c[...]
                pl.when(far == 1)(lambda: zcopy(sum_c, from_near, 2, mate).start())
                pl.when(far == 0)(lambda: zcopy(sum_c, from_far, 3, opposite).start())

    def mean_d():
        if grouped:
            @pl.when(adds)
            def _():
                zcopy(from_near, from_near, 2, mate).wait_recv()
                zcopy(from_far, from_far, 3, opposite).wait_recv()
                total_c[...] = (from_near[...] + from_far[...]) / groups
                zcopy(total_c, delta_out.at[other], 14, mate).start()
                zcopy(total_c, delta_out.at[other], 15, opposite).start()

    def mean_e():
        if grouped:
            @pl.when(is_lower)
            def _():
                pl.when(far == 1)(lambda: zcopy(delta_out.at[mine], delta_out.at[mine], 14, mate).wait_recv())
                pl.when(far == 0)(lambda: zcopy(delta_out.at[mine], delta_out.at[mine], 15, opposite).wait_recv())
                zcopy(delta_out.at[mine], delta_out.at[mine], 4, flip1).start()
                to_hearer(0, mine, 0).start()
                to_hearer(1, mine, 1).start()

    def mean_f():
        if grouped:
            @pl.when(is_lower)
            def _():
                zcopy(delta_out.at[other], delta_out.at[other], 4, flip1).wait_recv()
                half_done = delta_out.at[pl.ds(2 * b0, 2)]
                zcopy(half_done, half_done, 5, flip0).start()
                to_hearer(0, other, 2).start()
                to_hearer(1, other, 3).start()

    def mean_end():
        if grouped:
            @pl.when(is_lower)
            def _():
                half_done = delta_out.at[pl.ds(2 - 2 * b0, 2)]
                zcopy(half_done, half_done, 5, flip0).wait_recv()
                for copy in (zcopy(from_b, from_b, 0, flip0), zcopy(from_c, from_c, 1, flip1),
                             zcopy(sum_c, from_c, 4, flip1), zcopy(half_done, half_done, 5, flip0)):
                    copy.wait_send()
                pl.when(far == 1)(lambda: zcopy(sum_c, from_near, 2, mate).wait_send())
                pl.when(far == 0)(lambda: zcopy(sum_c, from_far, 3, opposite).wait_send())
                for k in range(4):
                    to_hearer(0, mine, k).wait_send()

            @pl.when(is_upper)
            def _():
                for i in range(4):
                    zcopy(delta_out.at[i], delta_out.at[i], 10 + i, flip1).wait_recv()
                for k in range(2):
                    to_holder(k).wait_send()

            @pl.when(adds)
            def _():
                zcopy(total_c, total_c, 14, mate).wait_send()
                zcopy(total_c, total_c, 15, opposite).wait_send()
        else:
            delta_out[...] = dd[...]

    def swap(k):
        return pltpu.make_async_remote_copy(
            src_ref=block(k, co), dst_ref=held(1, k), send_sem=xsem.at[k], recv_sem=xrsem.at[k],
            device_id=sib, device_id_type=MESH)

    def swap_start():
        for k in range(NF // 2):
            start(swap(k))

    def swap_end():
        for k in range(NF // 2):
            l_act[k].wait()
            swap(k).wait_recv()

    every, lo, hi = pl.ds(0, rows), pl.ds(0, half), pl.ds(half, half)
    first, but_first = pl.ds(0, edge), pl.ds(edge, rows - edge)
    last, but_last = pl.ds(rows - edge, edge), pl.ds(0, rows - edge)

    def give(q, kind, peer, shard, rng=every):
        ref = wg.at[q, shard, rng]
        send(ref, ref, q, kind, peer)

    def got(q, kind, shard, rng=every):
        arrived(wg.at[q, shard, rng], q, kind)

    def cast(q):
        l_params[q].wait()
        wg[q, chip(y, x)] = pv[:, columns(q)].astype(BF16)

    def own(q):
        if q > 0:
            cast(q)
        shard = chip(y, x)
        give(q, X_OWN, side, shard)
        give(q, YP_OWN, up, shard)
        give(q, YM_OWN, down, shard)

    def from_side(q):
        shard = chip(y, xo)
        got(q, X_OWN, shard)
        give(q, YP_X, up, shard, but_first)
        give(q, YM_X, down, shard, but_last)

    def from_down(q):
        shard = chip(ym, x)
        got(q, YP_OWN, shard)
        give(q, YP_F, up, shard, lo)
        give(q, X_P, side, shard, first)

    def from_up(q):
        shard = chip(yp, x)
        got(q, YM_OWN, shard)
        give(q, YM_F, down, shard, hi)
        give(q, X_M, side, shard, last)

    def far_lo(q):
        shard = chip(y2, x)
        got(q, YP_F, shard, lo)
        give(q, X_FA, side, shard, lo)

    def far_hi(q):
        shard = chip(y2, x)
        got(q, YM_F, shard, hi)
        give(q, X_FB, side, shard, hi)

    def product(q, chips):
        s = None
        for yy, xx in chips:
            k = chip(yy, xx)
            cols = pl.ds(pl.multiple_of(k * rows, rows), rows)
            d = jnp.dot(xk[:, cols], wg[q, k], preferred_element_type=F32)
            s = d if s is None else s + d
        return s

    def keys_a(q):
        acc[q] = product(q, [(y, x), (ym, x), (yp, x), (y, xo)])

    def keys_b(q):
        got(q, YP_X, chip(ym, xo), but_first)
        got(q, X_P, chip(ym, xo), first)
        got(q, YM_X, chip(yp, xo), but_last)
        got(q, X_M, chip(yp, xo), last)
        got(q, X_FA, chip(y2, xo), lo)
        got(q, X_FB, chip(y2, xo), hi)
        s = acc[q] + product(q, [(y2, x), (ym, xo), (yp, xo), (y2, xo)])
        acc[q] = s
        ksend[q] = s[tokens:]
        send(ksend.at[q], krecv.at[q], q, KEYS, sib)

    def residual(q):
        arrived(krecv.at[q], q, KEYS)
        keys = (acc[q, :tokens] + krecv[q]) * scale
        target = tv[:, columns(q)].astype(F32)
        rs[q, :tokens] = (live[...] * (keys - target) / total[0:1, 0:1]).astype(BF16)
        send(rs.at[q, pl.ds(0, tokens)], rs.at[q, pl.ds(tokens, tokens)], q, ROWS, sib)

    def turn(k):
        xt[k] = jnp.transpose(xk[:, k * rows:(k + 1) * rows])

    ready = set()

    def slope(q, yy, xx):
        if q not in ready:
            ready.add(q)
            arrived(rs.at[q, pl.ds(tokens, tokens)], q, ROWS)
        return jnp.dot(xt[chip(yy, xx)], rs[q], preferred_element_type=F32)

    def pass_on(q, buf, dst, rng, value, kind, peer):
        buf[q, rng] = value.astype(BF16)
        send(buf.at[q, rng], dst.at[q, rng], q, kind, peer)

    def sum_cross(q):
        pass_on(q, tx1, rx1, every, slope(q, y2, xo), X1, side)

    def sum_corner_up(q):
        ty1p[q] = slope(q, yp, xo).astype(BF16)
        send(ty1p.at[q, but_first], ry1p.at[q, but_first], q, Y1P, up)
        send(ty1p.at[q, first], rxep.at[q], q, XEP, side)

    def sum_corner_down(q):
        ty1m[q] = slope(q, ym, xo).astype(BF16)
        send(ty1m.at[q, but_last], ry1m.at[q, but_last], q, Y1M, down)
        send(ty1m.at[q, last], rxem.at[q], q, XEM, side)

    def sum_up(q):
        gown[q, 0] = slope(q, yp, x)
        pass_on(q, ty3p, ry3p, hi, gown[q, 0, hi], Y3PB, up)

    def sum_down(q):
        gown[q, 1] = slope(q, ym, x)
        pass_on(q, ty3m, ry3m, lo, gown[q, 1, lo], Y3MA, down)

    def part_far(q):
        gown[q, 2] = slope(q, y2, x)

    def part_side(q):
        gown[q, 3] = slope(q, y, xo)

    def part_own(q):
        gown[q, 4] = slope(q, y, x)

    def sum_far(q):
        arrived(rx1.at[q], q, X1)
        s = gown[q, 2] + rx1[q].astype(F32)
        pass_on(q, ty2p, ry2p, pl.ds(0, half), s[:half], Y2P, up)
        pass_on(q, ty2m, ry2m, pl.ds(0, half), s[half:], Y2M, down)

    def sum_side(q):
        arrived(ry1p.at[q, but_first], q, Y1P)
        arrived(ry1m.at[q, but_last], q, Y1M)
        zero = jnp.zeros((edge, cw), F32)
        s = gown[q, 3] + jnp.concatenate([zero, ry1p[q, but_first].astype(F32)])
        s = s + jnp.concatenate([ry1m[q, but_last].astype(F32), zero])
        pass_on(q, tx2, rx2, every, s, X2, side)

    def sum_up_far(q):
        arrived(ry2p.at[q], q, Y2P)
        arrived(rxep.at[q], q, XEP)
        s = gown[q, 0, lo] + ry2p[q].astype(F32)
        s = s + jnp.concatenate([rxep[q].astype(F32), jnp.zeros((half - edge, cw), F32)])
        pass_on(q, ty3p, ry3p, lo, s, Y3PA, up)

    def sum_down_far(q):
        arrived(ry2m.at[q], q, Y2M)
        arrived(rxem.at[q], q, XEM)
        s = gown[q, 1, hi] + ry2m[q].astype(F32)
        s = s + jnp.concatenate([jnp.zeros((half - edge, cw), F32), rxem[q].astype(F32)])
        pass_on(q, ty3m, ry3m, hi, s, Y3MB, down)

    def finish(q):
        arrived(rx2.at[q], q, X2)
        arrived(ry3p.at[q, hi], q, Y3PB)
        arrived(ry3m.at[q, lo], q, Y3MA)
        arrived(ry3p.at[q, lo], q, Y3PA)
        arrived(ry3m.at[q, hi], q, Y3MB)
        s = gown[q, 4] + rx2[q].astype(F32) + ry3p[q].astype(F32) + ry3m[q].astype(F32)
        grad_out[:, columns(q)] = s * scale

    cast(0)
    if grouped:
        pl.semaphore_wait(barrier, len(neighbours) + (1 - upper) * before + upper * (2 + far))

        @pl.when(is_lower)
        def _():
            pl.when(b0 == 0)(lambda: greet([flip0]))
            pl.when(b1 == 0)(lambda: greet([flip1]))
            greet([faced(1), faced(0)])
            pl.when(far == 0)(lambda: greet([opposite]))
            pl.when(b0 == 1)(lambda: greet([flip0]))
            pl.when(b1 == 1)(lambda: greet([flip1]))

        @pl.when(is_upper)
        def _():
            greet([faced(0), faced(1)])
            pl.when(far == 1)(lambda: greet([opposite]))
    else:
        pl.semaphore_wait(barrier, len(neighbours))
    own(0)
    count(0)
    swap_start()
    own(2)
    count(1)
    own(1)
    own(3)
    mean_start()
    mean_a()
    swap_end()
    turn(7)
    from_down(0)
    from_down(2)
    count(2)
    turn(4)
    from_up(0)
    turn(1)
    from_side(0)
    keys_a(0)
    turn(5)
    turn(2)
    turn(3)
    from_up(1)
    from_down(1)
    from_up(2)
    turn(6)
    turn(0)
    far_lo(0)
    far_hi(0)
    count(3)
    far_lo(2)
    from_down(3)
    from_side(1)
    keys_a(1)
    from_side(2)
    far_hi(1)
    keys_b(0)
    far_lo(1)
    from_side(3)
    far_hi(2)
    count(4)
    from_up(3)
    mean_b()
    l_tgt.wait()
    residual(0)
    far_lo(3)
    keys_a(2)
    sum_cross(0)
    keys_b(1)
    sum_down(0)
    keys_b(2)
    sum_corner_up(0)
    mean_c()
    residual(1)
    sum_corner_down(0)
    part_far(0)
    sum_far(0)
    far_hi(3)
    sum_up(0)
    mean_d()
    residual(2)
    sum_corner_down(1)
    sum_corner_up(1)
    sum_cross(1)
    keys_a(3)
    sum_corner_down(2)
    keys_b(3)
    sum_up_far(0)
    sum_cross(2)
    part_side(2)
    sum_corner_up(2)
    sum_down_far(0)
    part_far(1)
    residual(3)
    part_side(1)
    sum_far(1)
    sum_side(1)
    part_far(2)
    sum_up(1)
    part_own(0)
    sum_down(2)
    sum_far(2)
    sum_cross(3)
    part_own(1)
    sum_side(2)
    sum_down(1)
    part_own(3)
    sum_corner_up(3)
    mean_e()
    sum_corner_down(3)
    settle_gather()
    sum_down_far(2)
    part_far(3)
    sum_up(2)
    sum_up(3)
    part_side(0)
    sum_far(3)
    part_side(3)
    sum_side(0)
    sum_down(3)
    sum_up_far(2)
    sum_side(3)
    sum_down_far(1)
    mean_f()
    sum_up_far(1)
    sum_down_far(3)
    sum_up_far(3)
    part_own(2)
    finish(0)
    settle(0)
    finish(2)
    settle(2)
    finish(1)
    settle(1)
    finish(3)
    mean_end()
    for copy in l_later:
        copy.wait()
    for tag in list(sends):
        settle(tag)


def sync(activations, targets, token_ids, sync_fragment, params, adam_m, adam_v, anchor, momentum):
    tokens, width = activations.shape[1:]
    rows, kv = params.shape[1:]
    nq = kv // HEAD
    edge = EDGE * rows // 512
    piece = pltpu.VMEM((nq, rows, HEAD), BF16)
    part = pltpu.VMEM((nq, rows // 2, HEAD), BF16)
    thin = pltpu.VMEM((nq, edge, HEAD), BF16)
    quarter = pltpu.VMEM((rows // 4, HEAD), F32)
    full = jax.ShapeDtypeStruct((rows, kv), F32)
    hbm = pl.BlockSpec(memory_space=pltpu.HBM)
    vmem = pl.BlockSpec(memory_space=pltpu.VMEM)
    return pl.pallas_call(
        functools.partial(sync_kernel, float(width) ** (-0.5)),
        out_shape=(full, jax.ShapeDtypeStruct((4, rows // 4, HEAD), F32)) + (full,) * 5,
        in_specs=[hbm] * 9,
        out_specs=(vmem,) * 7,
        scratch_shapes=[
            pltpu.SMEM(sync_fragment.shape, jnp.int32),
            pltpu.VMEM((2 * tokens, width // 2), BF16),
            pltpu.VMEM((NF // 2, rows, 2 * tokens), BF16),
            pltpu.VMEM((tokens, kv), BF16),
            pltpu.VMEM((1, tokens), jnp.int32),
            pltpu.VMEM((tokens, HEAD), F32),
            pltpu.VMEM((8, HEAD), F32),
            pltpu.VMEM((nq, NF // 2, rows, HEAD), BF16),
            pltpu.VMEM((nq, 2 * tokens, HEAD), F32),
            pltpu.VMEM((nq, tokens, HEAD), F32),
            pltpu.VMEM((nq, tokens, HEAD), F32),
            pltpu.VMEM((nq, 2 * tokens, HEAD), BF16),
            pltpu.VMEM((nq, 5, rows, HEAD), F32),
            piece, piece, piece, thin, thin, part, part, piece, piece, piece,
            piece, piece, piece, part, part, piece, piece, piece,
            pltpu.VMEM((4, rows // 4, HEAD), F32),
            pltpu.VMEM((2, rows // 4, HEAD), F32), quarter,
            pltpu.VMEM((2, rows // 4, HEAD), F32), quarter, quarter, quarter, quarter,
            pltpu.VMEM((2, 2, rows // 4, HEAD), F32),
            pltpu.VMEM((4, 8, HEAD), F32),
            pltpu.VMEM((4, 8, HEAD), F32),
            pltpu.SemaphoreType.DMA((nq, KINDS)),
            pltpu.SemaphoreType.DMA((nq, KINDS)),
            pltpu.SemaphoreType.DMA((16,)),
            pltpu.SemaphoreType.DMA((16,)),
            pltpu.SemaphoreType.DMA((4,)),
            pltpu.SemaphoreType.DMA((4,)),
            pltpu.SemaphoreType.DMA((NF // 2,)),
            pltpu.SemaphoreType.DMA((NF // 2,)),
            pltpu.SemaphoreType.DMA((nq + 8 + NF // 2,)),
        ],
        compiler_params=pltpu.CompilerParams(
            collective_id=0, has_side_effects=True, vmem_limit_bytes=36 * 2**20
        ),
        cost_estimate=pl.CostEstimate(
            flops=4 * tokens * width * kv, bytes_accessed=2 * tokens * width + 12 * rows * kv, transcendentals=0
        ),
        name="sync",
    )(*[
        pltpu.with_memory_space_constraint(a, pltpu.HBM)
        for a in (activations, targets, token_ids, sync_fragment, params, adam_m, adam_v, anchor, momentum)
    ])


def update_kernel(steps, frag, grad, delta, params, adam_m, adam_v, anchor, momentum,
                  out_params, out_m, out_v, out_anchor, out_momentum,
                  new_params, new_m, new_v, new_anchor, new_momentum, sem):
    rows = grad.shape[0]
    size = rows // steps
    copies = []

    def store(src, dst):
        copy = pltpu.make_async_copy(src, dst, sem.at[len(copies)])
        copy.start()
        copies.append(copy)

    fragment = pl.ds(pl.multiple_of(frag[0] * HEAD, HEAD), HEAD)
    arriving = pl.ds(pl.multiple_of(frag[1] * HEAD, HEAD), HEAD)
    for i in range(steps):
        r = pl.ds(i * size, size)
        slope = grad[r]
        weight = params[r]
        first = beta_one * adam_m[r] + (1.0 - beta_one) * slope
        second = beta_two * adam_v[r] + (1.0 - beta_two) * slope * slope
        new_m[r] = first
        store(new_m.at[r], out_m.at[0, r])
        new_v[r] = second
        store(new_v.at[r], out_v.at[0, r])
        new_params[r] = weight - learn_rate * (first / (jnp.sqrt(second) + adam_epsilon) + decay_rate * weight)
        new_params[r, arriving] = merge_weight * new_params[r, arriving] + (1.0 - merge_weight) * anchor[r, arriving]
        store(new_params.at[r], out_params.at[0, r])
        new_anchor[r] = anchor[r]
        new_momentum[r] = momentum[r]
        change = delta[r]
        moment = outer_beta * momentum[r, fragment] + change
        new_momentum[r, fragment] = moment
        store(new_momentum.at[r], out_momentum.at[r])
        new_anchor[r, fragment] = anchor[r, fragment] - outer_rate * (change + outer_beta * moment)
        store(new_anchor.at[r], out_anchor.at[r])
    for copy in copies:
        copy.wait()


def update(frag, grad, delta, params, adam_m, adam_v, anchor, momentum, steps=4):
    rows, kv = grad.shape
    vmem = pl.BlockSpec(memory_space=pltpu.VMEM)
    hbm = pl.BlockSpec(memory_space=pltpu.HBM)
    return pl.pallas_call(
        functools.partial(update_kernel, steps),
        out_shape=[jax.ShapeDtypeStruct((1, rows, kv), F32)] * 3 + [jax.ShapeDtypeStruct((rows, kv), F32)] * 2,
        in_specs=[pl.BlockSpec(memory_space=pltpu.SMEM)] + [vmem] * 7,
        out_specs=[hbm] * 5,
        scratch_shapes=[pltpu.VMEM((rows, kv), F32)] * 5 + [pltpu.SemaphoreType.DMA((5 * steps,))],
        compiler_params=pltpu.CompilerParams(vmem_limit_bytes=16 * 2**20),
        name="update",
    )(frag, grad, delta, params, adam_m, adam_v, anchor, momentum)


def on_device(activations, targets, token_ids, sync_fragment, params, adam_m, adam_v, anchor, momentum):
    grad, delta, *held = sync(activations, targets, token_ids, sync_fragment, params, adam_m, adam_v, anchor, momentum)
    delta = delta.reshape(delta.shape[0] * delta.shape[1], delta.shape[2])
    return tuple(update(sync_fragment, grad, delta, *held))


def solution(mesh):
    worker = P("group", "fsdp", None)
    shared = P("fsdp", None)
    return jax.shard_map(
        on_device,
        mesh=mesh,
        in_specs=(worker, worker, P("group", "fsdp"), P(), worker, worker, worker, shared, shared),
        out_specs=(worker, worker, worker, shared, shared),
        check_vma=False,
    )
```

```python
import functools

import jax
import jax.numpy as jnp
from jax import lax
from jax.experimental import pallas as pl
from jax.experimental.pallas import tpu as pltpu
from jax.sharding import PartitionSpec as P

HEAD = 128
MESH = pl.DeviceIdType.MESH
F32 = jnp.float32
BF16 = jnp.bfloat16

beta_one = 0.9
beta_two = 0.999
learn_rate = 0.05
decay_rate = 0.1
adam_epsilon = 1e-08
outer_rate = 0.7
outer_beta = 0.9
merge_weight = 0.5

NF = 16
NZ = 8

EDGE = 80

(X_OWN, YP_OWN, YM_OWN, YP_X, YM_X, YP_F, YM_F, X_P, X_M, X_FA, X_FB, KEYS, ROWS,
 X1, Y1P, Y1M, XEP, XEM, Y2P, Y2M, Y3PB, Y3PA, Y3MA, Y3MB, X2) = range(25)
KINDS = 25


def sync_kernel(scale, act, tgt, ids, fragments, params, adam_m, adam_v, anchor, momentum,
                grad_out, delta_out, pv, mv, vv, av, uv,
                frag, xk, xt, tv, iv, live, total, wg, acc, ksend, krecv, rs, gown,
                rx1, ry1p, ry1m, rxep, rxem, ry2p, ry2m, ry3p, ry3m, rx2,
                tx1, ty1p, ty1m, ty2p, ty2m, ty3p, ty3m, tx2,
                dd, sum_b, sum_c, from_b, from_c, from_near, from_far, total_c, from_upper, cs, cr,
                ssem, rsem, zsem, zrsem, csem, crsem, xsem, xrsem, lsem):
    nq, _, rows, cw = wg.shape
    tokens = iv.shape[1]
    half = rows // 2
    edge = rxep.shape[1]
    g, me = lax.axis_index("group"), lax.axis_index("fsdp")
    y, x, c = me // 4, lax.rem(me // 2, 2), lax.rem(me, 2)
    z, far = lax.rem(g, NZ), g // NZ
    yp, ym, y2, xo, co = lax.rem(y + 1, 4), lax.rem(y + 3, 4), lax.rem(y + 2, 4), 1 - x, 1 - c
    groups = lax.axis_size("group")

    def at(yy, xx, cc):
        return yy * 4 + xx * 2 + cc

    def chip(yy, xx):
        return yy * 2 + xx

    sib, up, down, side = ((g, at(y, x, co)), (g, at(yp, x, c)), (g, at(ym, x, c)), (g, at(y, xo, c)))

    b0, b1, upper = lax.rem(z, 2), lax.rem(z // 2, 2), z // 4
    mine, other = 2 * b0 + b1, 2 * b0 + 1 - b1
    flip0, flip1 = (g + 1 - 2 * b0, me), (g + 2 - 4 * b1, me)
    facing = (1 - upper) * 4 + 2 * (1 - b1)
    mate, opposite = (far * NZ + facing + b0, me), ((1 - far) * NZ + facing + b0, me)
    before = b0 + b1

    def faced(k):
        return (far * NZ + facing + k, me)

    grouped = groups > 1
    is_lower, is_upper = upper == 0, upper == 1
    adds = upper * far == 1

    neighbours = [sib, up, down, side]
    barrier = pltpu.get_barrier_semaphore()

    def greet(peers):
        for peer in peers:
            pl.semaphore_signal(barrier, inc=1, device_id=peer, device_id_type=MESH)

    greet(neighbours)

    def columns(q):
        return slice(q * cw, (q + 1) * cw)

    def load(src, dst, k):
        copy = pltpu.make_async_copy(src, dst, lsem.at[k])
        copy.start()
        return copy

    l_params = [load(params.at[0, :, columns(q)], pv.at[:, columns(q)], q) for q in range(nq)]
    l_ids = load(ids, iv, nq)

    def block(k, core):
        return act.at[0, :, pl.ds(pl.multiple_of((2 * k + core) * rows, rows), rows)]

    def held(half, k):
        return xk.at[pl.ds(half * tokens, tokens), pl.ds(k * rows, rows)]

    l_act = [load(block(k, c), held(0, k), nq + 8 + k) for k in range(NF // 2)]
    l_tgt = load(tgt.at[0], tv, nq + 2)
    l_anchor = load(anchor, av, nq + 3)
    l_frag = load(fragments, frag, nq + 4)
    l_later = [load(adam_m.at[0], mv, nq + 5), load(adam_v.at[0], vv, nq + 6), load(momentum, uv, nq + 7)]

    sends = {}

    def start(copy, tag=None):
        copy.start()
        sends.setdefault(tag, []).append(copy)

    def settle(tag):
        for copy in sends.pop(tag, []):
            copy.wait_send()

    def settle_gather():
        for q in range(nq):
            settle(-1 - q)

    def remote(src, dst, q, kind, peer):
        return pltpu.make_async_remote_copy(
            src_ref=src, dst_ref=dst, send_sem=ssem.at[q, kind], recv_sem=rsem.at[q, kind],
            device_id=peer, device_id_type=MESH)

    def send(src, dst, q, kind, peer):
        start(remote(src, dst, q, kind, peer), q if kind >= X1 else -1 - q)

    def arrived(dst, q, kind):
        remote(dst, dst, q, kind, sib).wait_recv()

    y1, y3 = y + 1 - 2 * lax.rem(y, 2), 3 - y
    count_peers = [sib, side, (g, at(y1, x, c)), (g, at(y3, x, c))]

    def count_copy(k):
        return pltpu.make_async_remote_copy(
            src_ref=cs.at[k], dst_ref=cr.at[k], send_sem=csem.at[k], recv_sem=crsem.at[k],
            device_id=count_peers[k], device_id_type=MESH)

    def count(k):
        if k == 0:
            l_ids.wait()
            row = jnp.where(iv[...] != 0, 1.0, 0.0).astype(F32)
            live[...] = jnp.transpose(jnp.broadcast_to(row, (HEAD, tokens)))
            part = jnp.broadcast_to(jnp.sum(row), cs.shape[1:])
        else:
            count_copy(k - 1).wait_recv()
            part = cs[k - 1] + cr[k - 1]
        if k < 4:
            cs[k] = part
            start(count_copy(k))
        else:
            total[...] = part

    def zcopy(src, dst, k, peer):
        return pltpu.make_async_remote_copy(
            src_ref=src, dst_ref=dst, send_sem=zsem.at[k], recv_sem=zrsem.at[k],
            device_id=peer, device_id_type=MESH)

    def to_holder(k):
        return pltpu.make_async_remote_copy(
            src_ref=dd.at[pl.ds(2 * k, 2)], dst_ref=from_upper.at[b0], send_sem=zsem.at[6 + k], recv_sem=zrsem.at[6 + b0],
            device_id=faced(k), device_id_type=MESH)

    def to_hearer(k, quarter, i):
        return pltpu.make_async_remote_copy(
            src_ref=delta_out.at[quarter], dst_ref=delta_out.at[quarter], send_sem=zsem.at[8 + i], recv_sem=zrsem.at[10 + quarter],
            device_id=faced(k), device_id_type=MESH)

    def mean_start():
        l_anchor.wait()
        l_frag.wait()
        diff = av[:, columns(0)] - pv[:, columns(0)]
        for f in range(1, nq):
            diff = jnp.where(jnp.full(diff.shape, frag[0]) == f, av[:, columns(f)] - pv[:, columns(f)], diff)
        dd[...] = diff.reshape(dd.shape)
        if grouped:
            @pl.when(is_upper)
            def _():
                for k in range(2):
                    to_holder(k).start()

    def mean_a():
        if grouped:
            @pl.when(is_lower)
            def _():
                pl.semaphore_wait(barrier, 5 - before - far)
                zcopy(dd.at[pl.ds(2 - 2 * b0, 2)], from_b, 0, flip0).start()

    def mean_b():
        if grouped:
            @pl.when(is_lower)
            def _():
                zcopy(from_b, from_b, 0, flip0).wait_recv()
                s = dd[pl.ds(2 * b0, 2)] + from_b[...]
                for k in range(2):
                    zcopy(from_upper.at[k], from_upper.at[k], 6 + k, flip0).wait_recv()
                    s = s + from_upper[k]
                sum_b[...] = s
                zcopy(sum_b.at[1 - b1], from_c, 1, flip1).start()

    def mean_c():
        if grouped:
            @pl.when(is_lower)
            def _():
                zcopy(from_c, from_c, 1, flip1).wait_recv()
                sum_c[...] = sum_b[b1] + from_c[...]
                pl.when(far == 1)(lambda: zcopy(sum_c, from_near, 2, mate).start())
                pl.when(far == 0)(lambda: zcopy(sum_c, from_far, 3, opposite).start())

    def mean_d():
        if grouped:
            @pl.when(adds)
            def _():
                zcopy(from_near, from_near, 2, mate).wait_recv()
                zcopy(from_far, from_far, 3, opposite).wait_recv()
                total_c[...] = (from_near[...] + from_far[...]) / groups
                zcopy(total_c, delta_out.at[other], 14, mate).start()
                zcopy(total_c, delta_out.at[other], 15, opposite).start()

    def mean_e():
        if grouped:
            @pl.when(is_lower)
            def _():
                pl.when(far == 1)(lambda: zcopy(delta_out.at[mine], delta_out.at[mine], 14, mate).wait_recv())
                pl.when(far == 0)(lambda: zcopy(delta_out.at[mine], delta_out.at[mine], 15, opposite).wait_recv())
                zcopy(delta_out.at[mine], delta_out.at[mine], 4, flip1).start()
                to_hearer(0, mine, 0).start()
                to_hearer(1, mine, 1).start()

    def mean_f():
        if grouped:
            @pl.when(is_lower)
            def _():
                zcopy(delta_out.at[other], delta_out.at[other], 4, flip1).wait_recv()
                half_done = delta_out.at[pl.ds(2 * b0, 2)]
                zcopy(half_done, half_done, 5, flip0).start()
                to_hearer(0, other, 2).start()
                to_hearer(1, other, 3).start()

    def mean_end():
        if grouped:
            @pl.when(is_lower)
            def _():
                half_done = delta_out.at[pl.ds(2 - 2 * b0, 2)]
                zcopy(half_done, half_done, 5, flip0).wait_recv()
                for copy in (zcopy(from_b, from_b, 0, flip0), zcopy(from_c, from_c, 1, flip1),
                             zcopy(sum_c, from_c, 4, flip1), zcopy(half_done, half_done, 5, flip0)):
                    copy.wait_send()
                pl.when(far == 1)(lambda: zcopy(sum_c, from_near, 2, mate).wait_send())
                pl.when(far == 0)(lambda: zcopy(sum_c, from_far, 3, opposite).wait_send())
                for k in range(4):
                    to_hearer(0, mine, k).wait_send()

            @pl.when(is_upper)
            def _():
                for i in range(4):
                    zcopy(delta_out.at[i], delta_out.at[i], 10 + i, flip1).wait_recv()
                for k in range(2):
                    to_holder(k).wait_send()

            @pl.when(adds)
            def _():
                zcopy(total_c, total_c, 14, mate).wait_send()
                zcopy(total_c, total_c, 15, opposite).wait_send()
        else:
            delta_out[...] = dd[...]

    def swap(k):
        return pltpu.make_async_remote_copy(
            src_ref=block(k, co), dst_ref=held(1, k), send_sem=xsem.at[k], recv_sem=xrsem.at[k],
            device_id=sib, device_id_type=MESH)

    def swap_start():
        for k in range(NF // 2):
            start(swap(k))

    def swap_end():
        for k in range(NF // 2):
            l_act[k].wait()
            swap(k).wait_recv()

    every, lo, hi = pl.ds(0, rows), pl.ds(0, half), pl.ds(half, half)
    first, but_first = pl.ds(0, edge), pl.ds(edge, rows - edge)
    last, but_last = pl.ds(rows - edge, edge), pl.ds(0, rows - edge)

    def give(q, kind, peer, shard, rng=every):
        ref = wg.at[q, shard, rng]
        send(ref, ref, q, kind, peer)

    def got(q, kind, shard, rng=every):
        arrived(wg.at[q, shard, rng], q, kind)

    def cast(q):
        l_params[q].wait()
        wg[q, chip(y, x)] = pv[:, columns(q)].astype(BF16)

    def own(q):
        if q > 0:
            cast(q)
        shard = chip(y, x)
        give(q, X_OWN, side, shard)
        give(q, YP_OWN, up, shard)
        give(q, YM_OWN, down, shard)

    def from_side(q):
        shard = chip(y, xo)
        got(q, X_OWN, shard)
        give(q, YP_X, up, shard, but_first)
        give(q, YM_X, down, shard, but_last)

    def from_down(q):
        shard = chip(ym, x)
        got(q, YP_OWN, shard)
        give(q, YP_F, up, shard, lo)
        give(q, X_P, side, shard, first)

    def from_up(q):
        shard = chip(yp, x)
        got(q, YM_OWN, shard)
        give(q, YM_F, down, shard, hi)
        give(q, X_M, side, shard, last)

    def far_lo(q):
        shard = chip(y2, x)
        got(q, YP_F, shard, lo)
        give(q, X_FA, side, shard, lo)

    def far_hi(q):
        shard = chip(y2, x)
        got(q, YM_F, shard, hi)
        give(q, X_FB, side, shard, hi)

    def product(q, chips):
        s = None
        for yy, xx in chips:
            k = chip(yy, xx)
            cols = pl.ds(pl.multiple_of(k * rows, rows), rows)
            d = jnp.dot(xk[:, cols], wg[q, k], preferred_element_type=F32)
            s = d if s is None else s + d
        return s

    def keys_a(q):
        acc[q] = product(q, [(y, x), (ym, x), (yp, x), (y, xo)])

    def keys_b(q):
        got(q, YP_X, chip(ym, xo), but_first)
        got(q, X_P, chip(ym, xo), first)
        got(q, YM_X, chip(yp, xo), but_last)
        got(q, X_M, chip(yp, xo), last)
        got(q, X_FA, chip(y2, xo), lo)
        got(q, X_FB, chip(y2, xo), hi)
        s = acc[q] + product(q, [(y2, x), (ym, xo), (yp, xo), (y2, xo)])
        acc[q] = s
        ksend[q] = s[tokens:]
        send(ksend.at[q], krecv.at[q], q, KEYS, sib)

    def residual(q):
        arrived(krecv.at[q], q, KEYS)
        keys = (acc[q, :tokens] + krecv[q]) * scale
        target = tv[:, columns(q)].astype(F32)
        rs[q, :tokens] = (live[...] * (keys - target) / total[0:1, 0:1]).astype(BF16)
        send(rs.at[q, pl.ds(0, tokens)], rs.at[q, pl.ds(tokens, tokens)], q, ROWS, sib)

    def turn(k):
        xt[k] = jnp.transpose(xk[:, k * rows:(k + 1) * rows])

    ready = set()

    def slope(q, yy, xx):
        if q not in ready:
            ready.add(q)
            arrived(rs.at[q, pl.ds(tokens, tokens)], q, ROWS)
        return jnp.dot(xt[chip(yy, xx)], rs[q], preferred_element_type=F32)

    def pass_on(q, buf, dst, rng, value, kind, peer):
        buf[q, rng] = value.astype(BF16)
        send(buf.at[q, rng], dst.at[q, rng], q, kind, peer)

    def sum_cross(q):
        pass_on(q, tx1, rx1, every, slope(q, y2, xo), X1, side)

    def sum_corner_up(q):
        ty1p[q] = slope(q, yp, xo).astype(BF16)
        send(ty1p.at[q, but_first], ry1p.at[q, but_first], q, Y1P, up)
        send(ty1p.at[q, first], rxep.at[q], q, XEP, side)

    def sum_corner_down(q):
        ty1m[q] = slope(q, ym, xo).astype(BF16)
        send(ty1m.at[q, but_last], ry1m.at[q, but_last], q, Y1M, down)
        send(ty1m.at[q, last], rxem.at[q], q, XEM, side)

    def sum_up(q):
        gown[q, 0] = slope(q, yp, x)
        pass_on(q, ty3p, ry3p, hi, gown[q, 0, hi], Y3PB, up)

    def sum_down(q):
        gown[q, 1] = slope(q, ym, x)
        pass_on(q, ty3m, ry3m, lo, gown[q, 1, lo], Y3MA, down)

    def part_far(q):
        gown[q, 2] = slope(q, y2, x)

    def part_side(q):
        gown[q, 3] = slope(q, y, xo)

    def part_own(q):
        gown[q, 4] = slope(q, y, x)

    def sum_far(q):
        arrived(rx1.at[q], q, X1)
        s = gown[q, 2] + rx1[q].astype(F32)
        pass_on(q, ty2p, ry2p, pl.ds(0, half), s[:half], Y2P, up)
        pass_on(q, ty2m, ry2m, pl.ds(0, half), s[half:], Y2M, down)

    def sum_side(q):
        arrived(ry1p.at[q, but_first], q, Y1P)
        arrived(ry1m.at[q, but_last], q, Y1M)
        zero = jnp.zeros((edge, cw), F32)
        s = gown[q, 3] + jnp.concatenate([zero, ry1p[q, but_first].astype(F32)])
        s = s + jnp.concatenate([ry1m[q, but_last].astype(F32), zero])
        pass_on(q, tx2, rx2, every, s, X2, side)

    def sum_up_far(q):
        arrived(ry2p.at[q], q, Y2P)
        arrived(rxep.at[q], q, XEP)
        s = gown[q, 0, lo] + ry2p[q].astype(F32)
        s = s + jnp.concatenate([rxep[q].astype(F32), jnp.zeros((half - edge, cw), F32)])
        pass_on(q, ty3p, ry3p, lo, s, Y3PA, up)

    def sum_down_far(q):
        arrived(ry2m.at[q], q, Y2M)
        arrived(rxem.at[q], q, XEM)
        s = gown[q, 1, hi] + ry2m[q].astype(F32)
        s = s + jnp.concatenate([jnp.zeros((half - edge, cw), F32), rxem[q].astype(F32)])
        pass_on(q, ty3m, ry3m, hi, s, Y3MB, down)

    def finish(q):
        arrived(rx2.at[q], q, X2)
        arrived(ry3p.at[q, hi], q, Y3PB)
        arrived(ry3m.at[q, lo], q, Y3MA)
        arrived(ry3p.at[q, lo], q, Y3PA)
        arrived(ry3m.at[q, hi], q, Y3MB)
        s = gown[q, 4] + rx2[q].astype(F32) + ry3p[q].astype(F32) + ry3m[q].astype(F32)
        grad_out[:, columns(q)] = s * scale

    cast(0)
    if grouped:
        pl.semaphore_wait(barrier, len(neighbours) + (1 - upper) * before + upper * (2 + far))

        @pl.when(is_lower)
        def _():
            pl.when(b0 == 0)(lambda: greet([flip0]))
            pl.when(b1 == 0)(lambda: greet([flip1]))
            greet([faced(1), faced(0)])
            pl.when(far == 0)(lambda: greet([opposite]))
            pl.when(b0 == 1)(lambda: greet([flip0]))
            pl.when(b1 == 1)(lambda: greet([flip1]))

        @pl.when(is_upper)
        def _():
            greet([faced(0), faced(1)])
            pl.when(far == 1)(lambda: greet([opposite]))
    else:
        pl.semaphore_wait(barrier, len(neighbours))
    own(0)
    count(0)
    swap_start()
    own(2)
    count(1)
    own(1)
    own(3)
    mean_start()
    swap_end()
    turn(7)
    from_down(0)
    from_down(2)
    count(2)
    turn(4)
    from_up(0)
    turn(1)
    from_side(0)
    mean_a()
    keys_a(0)
    turn(5)
    turn(2)
    turn(3)
    from_up(1)
    from_down(1)
    from_up(2)
    turn(6)
    turn(0)
    far_lo(0)
    far_hi(0)
    count(3)
    far_lo(2)
    from_down(3)
    from_side(1)
    keys_a(1)
    from_side(2)
    far_hi(1)
    keys_b(0)
    far_lo(1)
    from_side(3)
    far_hi(2)
    count(4)
    from_up(3)
    mean_b()
    l_tgt.wait()
    residual(0)
    far_lo(3)
    keys_a(2)
    sum_cross(0)
    keys_b(1)
    sum_down(0)
    keys_b(2)
    sum_corner_up(0)
    mean_c()
    residual(1)
    sum_corner_down(0)
    part_far(0)
    sum_far(0)
    far_hi(3)
    sum_up(0)
    mean_d()
    residual(2)
    sum_corner_down(1)
    sum_corner_up(1)
    sum_cross(1)
    keys_a(3)
    sum_corner_down(2)
    keys_b(3)
    sum_up_far(0)
    sum_cross(2)
    part_side(2)
    sum_corner_up(2)
    sum_down_far(0)
    part_far(1)
    residual(3)
    part_side(1)
    sum_far(1)
    sum_side(1)
    part_far(2)
    sum_up(1)
    part_own(0)
    sum_down(2)
    sum_far(2)
    sum_cross(3)
    part_own(1)
    sum_side(2)
    sum_down(1)
    part_own(3)
    sum_corner_up(3)
    mean_e()
    sum_corner_down(3)
    settle_gather()
    sum_down_far(2)
    part_far(3)
    sum_up(2)
    sum_up(3)
    part_side(0)
    sum_far(3)
    part_side(3)
    sum_side(0)
    sum_down(3)
    sum_up_far(2)
    sum_side(3)
    sum_down_far(1)
    mean_f()
    sum_up_far(1)
    sum_down_far(3)
    sum_up_far(3)
    part_own(2)
    finish(0)
    settle(0)
    finish(2)
    settle(2)
    finish(1)
    settle(1)
    finish(3)
    mean_end()
    for copy in l_later:
        copy.wait()
    for tag in list(sends):
        settle(tag)


def sync(activations, targets, token_ids, sync_fragment, params, adam_m, adam_v, anchor, momentum):
    tokens, width = activations.shape[1:]
    rows, kv = params.shape[1:]
    nq = kv // HEAD
    edge = EDGE * rows // 512
    piece = pltpu.VMEM((nq, rows, HEAD), BF16)
    part = pltpu.VMEM((nq, rows // 2, HEAD), BF16)
    thin = pltpu.VMEM((nq, edge, HEAD), BF16)
    quarter = pltpu.VMEM((rows // 4, HEAD), F32)
    full = jax.ShapeDtypeStruct((rows, kv), F32)
    hbm = pl.BlockSpec(memory_space=pltpu.HBM)
    vmem = pl.BlockSpec(memory_space=pltpu.VMEM)
    return pl.pallas_call(
        functools.partial(sync_kernel, float(width) ** (-0.5)),
        out_shape=(full, jax.ShapeDtypeStruct((4, rows // 4, HEAD), F32)) + (full,) * 5,
        in_specs=[hbm] * 9,
        out_specs=(vmem,) * 7,
        scratch_shapes=[
            pltpu.SMEM(sync_fragment.shape, jnp.int32),
            pltpu.VMEM((2 * tokens, width // 2), BF16),
            pltpu.VMEM((NF // 2, rows, 2 * tokens), BF16),
            pltpu.VMEM((tokens, kv), BF16),
            pltpu.VMEM((1, tokens), jnp.int32),
            pltpu.VMEM((tokens, HEAD), F32),
            pltpu.VMEM((8, HEAD), F32),
            pltpu.VMEM((nq, NF // 2, rows, HEAD), BF16),
            pltpu.VMEM((nq, 2 * tokens, HEAD), F32),
            pltpu.VMEM((nq, tokens, HEAD), F32),
            pltpu.VMEM((nq, tokens, HEAD), F32),
            pltpu.VMEM((nq, 2 * tokens, HEAD), BF16),
            pltpu.VMEM((nq, 5, rows, HEAD), F32),
            piece, piece, piece, thin, thin, part, part, piece, piece, piece,
            piece, piece, piece, part, part, piece, piece, piece,
            pltpu.VMEM((4, rows // 4, HEAD), F32),
            pltpu.VMEM((2, rows // 4, HEAD), F32), quarter,
            pltpu.VMEM((2, rows // 4, HEAD), F32), quarter, quarter, quarter, quarter,
            pltpu.VMEM((2, 2, rows // 4, HEAD), F32),
            pltpu.VMEM((4, 8, HEAD), F32),
            pltpu.VMEM((4, 8, HEAD), F32),
            pltpu.SemaphoreType.DMA((nq, KINDS)),
            pltpu.SemaphoreType.DMA((nq, KINDS)),
            pltpu.SemaphoreType.DMA((16,)),
            pltpu.SemaphoreType.DMA((16,)),
            pltpu.SemaphoreType.DMA((4,)),
            pltpu.SemaphoreType.DMA((4,)),
            pltpu.SemaphoreType.DMA((NF // 2,)),
            pltpu.SemaphoreType.DMA((NF // 2,)),
            pltpu.SemaphoreType.DMA((nq + 8 + NF // 2,)),
        ],
        compiler_params=pltpu.CompilerParams(
            collective_id=0, has_side_effects=True, vmem_limit_bytes=36 * 2**20
        ),
        cost_estimate=pl.CostEstimate(
            flops=4 * tokens * width * kv, bytes_accessed=2 * tokens * width + 12 * rows * kv, transcendentals=0
        ),
        name="sync",
    )(*[
        pltpu.with_memory_space_constraint(a, pltpu.HBM)
        for a in (activations, targets, token_ids, sync_fragment, params, adam_m, adam_v, anchor, momentum)
    ])


def update_kernel(steps, frag, grad, delta, params, adam_m, adam_v, anchor, momentum,
                  out_params, out_m, out_v, out_anchor, out_momentum,
                  new_params, new_m, new_v, new_anchor, new_momentum, sem):
    rows = grad.shape[0]
    size = rows // steps
    copies = []

    def store(src, dst):
        copy = pltpu.make_async_copy(src, dst, sem.at[len(copies)])
        copy.start()
        copies.append(copy)

    fragment = pl.ds(pl.multiple_of(frag[0] * HEAD, HEAD), HEAD)
    arriving = pl.ds(pl.multiple_of(frag[1] * HEAD, HEAD), HEAD)
    for i in range(steps):
        r = pl.ds(i * size, size)
        slope = grad[r]
        weight = params[r]
        first = beta_one * adam_m[r] + (1.0 - beta_one) * slope
        second = beta_two * adam_v[r] + (1.0 - beta_two) * slope * slope
        new_m[r] = first
        store(new_m.at[r], out_m.at[0, r])
        new_v[r] = second
        store(new_v.at[r], out_v.at[0, r])
        new_params[r] = weight - learn_rate * (first / (jnp.sqrt(second) + adam_epsilon) + decay_rate * weight)
        new_params[r, arriving] = merge_weight * new_params[r, arriving] + (1.0 - merge_weight) * anchor[r, arriving]
        store(new_params.at[r], out_params.at[0, r])
        new_anchor[r] = anchor[r]
        new_momentum[r] = momentum[r]
        change = delta[r]
        moment = outer_beta * momentum[r, fragment] + change
        new_momentum[r, fragment] = moment
        store(new_momentum.at[r], out_momentum.at[r])
        new_anchor[r, fragment] = anchor[r, fragment] - outer_rate * (change + outer_beta * moment)
        store(new_anchor.at[r], out_anchor.at[r])
    for copy in copies:
        copy.wait()


def update(frag, grad, delta, params, adam_m, adam_v, anchor, momentum, steps=4):
    rows, kv = grad.shape
    vmem = pl.BlockSpec(memory_space=pltpu.VMEM)
    hbm = pl.BlockSpec(memory_space=pltpu.HBM)
    return pl.pallas_call(
        functools.partial(update_kernel, steps),
        out_shape=[jax.ShapeDtypeStruct((1, rows, kv), F32)] * 3 + [jax.ShapeDtypeStruct((rows, kv), F32)] * 2,
        in_specs=[pl.BlockSpec(memory_space=pltpu.SMEM)] + [vmem] * 7,
        out_specs=[hbm] * 5,
        scratch_shapes=[pltpu.VMEM((rows, kv), F32)] * 5 + [pltpu.SemaphoreType.DMA((5 * steps,))],
        compiler_params=pltpu.CompilerParams(vmem_limit_bytes=16 * 2**20),
        name="update",
    )(frag, grad, delta, params, adam_m, adam_v, anchor, momentum)


def on_device(activations, targets, token_ids, sync_fragment, params, adam_m, adam_v, anchor, momentum):
    grad, delta, *held = sync(activations, targets, token_ids, sync_fragment, params, adam_m, adam_v, anchor, momentum)
    delta = delta.reshape(delta.shape[0] * delta.shape[1], delta.shape[2])
    return tuple(update(sync_fragment, grad, delta, *held))


def solution(mesh):
    worker = P("group", "fsdp", None)
    shared = P("fsdp", None)
    return jax.shard_map(
        on_device,
        mesh=mesh,
        in_specs=(worker, worker, P("group", "fsdp"), P(), worker, worker, worker, shared, shared),
        out_specs=(worker, worker, worker, shared, shared),
        check_vma=False,
    )
```
